256 devices in a mesh: ctx: 64 (over x, y, z_hi), pipe: 4 (over z_lo, core).
Axes of the slice: x: 4, y: 4, z: 8 (z_hi: 4, z_lo: 2; z = z_hi * 2 + z_lo), core: 2. Of those that a mesh axis runs over, the one named last changes fastest.
Arguments:
- q_heads: bfloat16 [4, 24576, 4096], P('pipe', 'ctx'), may hold values from -6 to 6
- key_value_heads: bfloat16 [4, 24576, 1024], P('pipe', 'ctx'), may hold values from -6 to 6
- grad_out: bfloat16 [4, 24576, 4096], P('pipe', 'ctx'), may hold values from -6 to 6
- log_norm: float32 [4, 32, 24576], P('pipe', None, 'ctx'), may hold values from 2 to 4
- row_delta: float32 [4, 32, 24576], P('pipe', None, 'ctx'), may hold values from -24 to 24
- doc_starts: int32 [4, 64, 4], P('pipe'), may hold values from 0 to 383, as said below
- partner: int32 [4, 64], P('pipe'), may hold values from 0 to 63, as said below
Outputs:
- recv_grads: bfloat16 [4, 24576, 5120], P('pipe', 'ctx')
The draws below stay inside these ranges and needn't reach their ends.
Inputs may be any that keep to these rules, and one draw needn't show every extreme that they name: doc_starts[s, c] rises strictly and begins with 0. The first piece of block c continues the last piece of block partner[s, c] and comes after it in the document. The last piece of every block holds at most 256 rows, exactly 256 in some block of every section. partner[s, partner[s, c]] = c, and partner[s, c] differs from c in exactly one binary digit.
All inputs are finite; a program needn't handle non-finite values.
Results may differ from the reference program's by a relative error of at most 0.0056.
Values may be sent and summed in bfloat16 or wider, within the bound.
No kernel may reach another device: no remote copies, remote signals or barrier semaphores. Data moves between devices by JAX's collectives and lax.ppermute only.
A program may use at most 128 MiB of HBM per device.

```python
import jax
import jax.numpy as jnp
from jax import lax

HEAD_SIZE = 128
QUERY_HEADS = 32
KEY_VALUE_HEADS = 4
TOK_DEV = 384
EDGE = 256
DOCS = 4
RELAY_SECTIONS = 4
SHARDS = 64
PACKED_TOKENS = 24576


def draw_doc_starts(key, part):
    key = jax.random.fold_in(key, 11)
    subkeys = jax.random.split(key, 5)
    grid_shape = (RELAY_SECTIONS, SHARDS)
    tail_rows = 1 + jax.random.randint(subkeys[0], grid_shape, 0, EDGE)
    longest = jax.random.randint(subkeys[1], (RELAY_SECTIONS, 1), 0, SHARDS)
    shortest = (longest + 1 + jax.random.randint(subkeys[2], (RELAY_SECTIONS, 1), 0, SHARDS - 1)) % SHARDS
    column = jnp.arange(SHARDS, dtype=jnp.int32)[None, :]
    tail_rows = jnp.where(column == longest, EDGE, jnp.where(column == shortest, 1, tail_rows))
    before = TOK_DEV - tail_rows
    middle = DOCS - 2
    first_rows = 1 + jax.random.randint(subkeys[3], grid_shape, 0, 1 << 30) % (before - middle)
    remaining = before - first_rows
    cut_values = jax.random.randint(subkeys[4], grid_shape + (DOCS - 3,), 0, 1 << 30) % (remaining - middle + 1)[:, :, None]
    cut_values = jnp.sort(cut_values, axis=2) + 1 + jnp.arange(DOCS - 3, dtype=jnp.int32)[None, None, :]
    offsets = jnp.concatenate([jnp.zeros(grid_shape + (1,), jnp.int32), first_rows[:, :, None], first_rows[:, :, None] + cut_values, before[:, :, None]], axis=2)
    return offsets.astype(jnp.int32)


def draw_partner(key, part):
    key = jax.random.fold_in(key, 23)
    subkeys = jax.random.split(key, 2)
    bit_count = int(SHARDS).bit_length() - 1
    column = jnp.arange(SHARDS, dtype=jnp.int32)[None, :]
    middle_bit = 1 + jax.random.randint(subkeys[0], (RELAY_SECTIONS, 1), 0, bit_count - 2)
    top_mask = 1 << bit_count - 1
    middle_mask = jnp.left_shift(jnp.ones((RELAY_SECTIONS, 1), jnp.int32), middle_bit)
    block_id = jnp.bitwise_and(column, jnp.bitwise_not(jnp.bitwise_or(middle_mask, 1 + top_mask)))
    selector = jax.random.randint(subkeys[1], (RELAY_SECTIONS, SHARDS), 0, 3)
    picked = jnp.take_along_axis(selector, block_id, axis=1)
    flip_mask = jnp.where(picked == 0, 1, jnp.where(picked == 1, middle_mask, top_mask))
    return jnp.bitwise_xor(column, flip_mask).astype(jnp.int32)


def level_of(rng, dims, shards, least, top_value):
    gain = 1.0
    for axis_at, blocks in shards:
        draws = jax.random.uniform(jax.random.fold_in(jax.random.fold_in(rng, 6), axis_at), (blocks,), jnp.float32, least / len(shards), top_value / len(shards))
        gain = gain * jnp.repeat(jnp.exp(draws), dims[axis_at] // blocks).reshape((-1,) + (1,) * (len(dims) - 1 - axis_at))
    return gain


def noise(key, shape, deviation, most, cuts=(), kind=jnp.bfloat16):
    loudness = level_of(key, shape, cuts, -0.22, 0.18) if cuts else 1.0
    values = jax.random.normal(key, shape, jnp.float32) * deviation * loudness
    return jnp.minimum(jnp.maximum(values, -most), most).astype(kind)


def setup_inputs(seed: int = 0) -> dict:
    keys = jax.random.split(jax.random.key(seed), 8)
    q_heads = noise(keys[0], (RELAY_SECTIONS, PACKED_TOKENS, QUERY_HEADS * HEAD_SIZE), 1.0, 6.0, ((0, 4), (1, 64)))
    key_value_heads = noise(keys[1], (RELAY_SECTIONS, PACKED_TOKENS, 2 * KEY_VALUE_HEADS * HEAD_SIZE), 1.0, 6.0, ((0, 4), (1, 64)))
    grad_out = noise(keys[2], (RELAY_SECTIONS, PACKED_TOKENS, QUERY_HEADS * HEAD_SIZE), 1.0, 6.0, ((0, 4), (1, 64)))
    log_norm = jnp.clip(2.0 + 2.0 * jax.random.uniform(keys[3], (RELAY_SECTIONS, QUERY_HEADS, PACKED_TOKENS), jnp.float32) ** level_of(keys[3], (RELAY_SECTIONS, QUERY_HEADS, PACKED_TOKENS), ((0, 4), (2, 64)), -0.2, 0.2), 2.0, 4.0)
    row_delta = noise(keys[4], (RELAY_SECTIONS, QUERY_HEADS, PACKED_TOKENS), 4.0, 24.0, ((0, 4), (2, 64)), jnp.float32)
    doc_starts = draw_doc_starts(jax.random.fold_in(keys[7], 71), 0)
    partner = draw_partner(jax.random.fold_in(keys[7], 71), 0)
    return {"q_heads": q_heads, "key_value_heads": key_value_heads, "grad_out": grad_out, "log_norm": log_norm, "row_delta": row_delta, "doc_starts": doc_starts, "partner": partner}


def doc_index(starts, row_count):
    positions = jnp.arange(row_count, dtype=jnp.int32)
    return jnp.sum((starts[1:][None, :] <= positions[:, None]).astype(jnp.int32), axis=1)


def pick_rows(source, chosen):
    return source[chosen]


def block_grads(operands):
    queries, outgrads, keyvals, lognorms, deltas, starts, remote_rows, remote_start = operands
    group_list = QUERY_HEADS // KEY_VALUE_HEADS
    score_scale = HEAD_SIZE ** -0.5
    rows_of_keys = jnp.concatenate([remote_rows, keyvals], axis=0)
    query_document = doc_index(starts, TOK_DEV)
    positions = jnp.arange(TOK_DEV, dtype=jnp.int32)
    edge_live = (TOK_DEV - EDGE + jnp.arange(EDGE, dtype=jnp.int32)) >= remote_start
    key_document = jnp.concatenate([jnp.where(edge_live, 0, -1).astype(jnp.int32), query_document])
    key_position = jnp.concatenate([jnp.full((EDGE,), -1, jnp.int32), positions])
    allowed = (query_document[:, None] == key_document[None, :]) & (key_position[None, :] <= positions[:, None])
    query_parts = []
    key_parts = []
    value_parts = []
    for index_of_group in range(KEY_VALUE_HEADS):
        first_head = index_of_group * group_list
        query_group = queries[:, first_head * HEAD_SIZE:(first_head + group_list) * HEAD_SIZE].reshape(TOK_DEV, group_list, HEAD_SIZE).astype(jnp.float32)
        grad_group = outgrads[:, first_head * HEAD_SIZE:(first_head + group_list) * HEAD_SIZE].reshape(TOK_DEV, group_list, HEAD_SIZE).astype(jnp.float32)
        key_group = rows_of_keys[:, index_of_group * HEAD_SIZE:(index_of_group + 1) * HEAD_SIZE].astype(jnp.float32)
        group_of_values = rows_of_keys[:, (KEY_VALUE_HEADS + index_of_group) * HEAD_SIZE:(KEY_VALUE_HEADS + index_of_group + 1) * HEAD_SIZE].astype(jnp.float32)
        scores = jnp.einsum("qhd,kd->hqk", query_group, key_group) * score_scale
        weights = jnp.where(allowed[None], jnp.exp(scores - lognorms[first_head:first_head + group_list, :, None]), 0.0)
        weights_low = lax.optimization_barrier(weights.astype(jnp.bfloat16)).astype(jnp.float32)
        value_parts.append(jnp.einsum("hqk,qhd->kd", weights_low, grad_group))
        prob_grad = jnp.einsum("qhd,kd->hqk", grad_group, group_of_values)
        score_grad = weights * (prob_grad - deltas[first_head:first_head + group_list, :, None])
        score_grad = lax.optimization_barrier(score_grad.astype(jnp.bfloat16)).astype(jnp.float32)
        query_parts.append(jnp.einsum("hqk,kd->qhd", score_grad, key_group).reshape(TOK_DEV, group_list * HEAD_SIZE) * score_scale)
        key_parts.append(jnp.einsum("hqk,qhd->kd", score_grad, query_group) * score_scale)
    query_grad = jnp.concatenate(query_parts, axis=1).astype(jnp.bfloat16)
    keyval_part = jnp.concatenate(key_parts + value_parts, axis=1)
    return query_grad, keyval_part[EDGE:], keyval_part[:EDGE].astype(jnp.bfloat16)


def reference(q_heads, key_value_heads, grad_out, log_norm, row_delta, doc_starts, partner):
    width_size = 2 * KEY_VALUE_HEADS * HEAD_SIZE
    blocks = RELAY_SECTIONS * SHARDS
    queries = q_heads.reshape(blocks, TOK_DEV, QUERY_HEADS * HEAD_SIZE)
    outgrads = grad_out.reshape(blocks, TOK_DEV, QUERY_HEADS * HEAD_SIZE)
    keyvals = key_value_heads.reshape(RELAY_SECTIONS, SHARDS, TOK_DEV, width_size)
    edge_rows = keyvals[:, :, TOK_DEV - EDGE:, :]
    remote_rows = jax.vmap(pick_rows)(edge_rows, partner)
    remote_start = jax.vmap(pick_rows)(doc_starts[:, :, DOCS - 1], partner)
    lognorms = log_norm.reshape(RELAY_SECTIONS, QUERY_HEADS, SHARDS, TOK_DEV).transpose(0, 2, 1, 3).reshape(blocks, QUERY_HEADS, TOK_DEV)
    deltas = row_delta.reshape(RELAY_SECTIONS, QUERY_HEADS, SHARDS, TOK_DEV).transpose(0, 2, 1, 3).reshape(blocks, QUERY_HEADS, TOK_DEV)
    operands = (queries, outgrads, keyvals.reshape(blocks, TOK_DEV, width_size), lognorms, deltas,
                doc_starts.reshape(blocks, DOCS), remote_rows.reshape(blocks, EDGE, width_size), remote_start.reshape(blocks))
    query_grad, local_part, edge_partial = lax.map(block_grads, operands)
    returned = jax.vmap(pick_rows)(edge_partial.reshape(RELAY_SECTIONS, SHARDS, EDGE, width_size), partner)
    local_part = local_part.reshape(RELAY_SECTIONS, SHARDS, TOK_DEV, width_size)
    tail_rows = local_part[:, :, TOK_DEV - EDGE:, :] + returned.astype(jnp.float32)
    keyval_grad = jnp.concatenate([local_part[:, :, :TOK_DEV - EDGE, :], tail_rows], axis=2).astype(jnp.bfloat16)
    joined_result = jnp.concatenate([query_grad.reshape(RELAY_SECTIONS, SHARDS, TOK_DEV, QUERY_HEADS * HEAD_SIZE), keyval_grad], axis=3)
    joined_result = joined_result.reshape(RELAY_SECTIONS, PACKED_TOKENS, (QUERY_HEADS + 2 * KEY_VALUE_HEADS) * HEAD_SIZE)
    return jnp.roll(joined_result, -1, axis=0)
```

```python
import functools
import math

import jax
import jax.numpy as jnp
from jax import lax
from jax.experimental import pallas as pl
from jax.experimental.pallas import tpu as pltpu
from jax.sharding import PartitionSpec as P

HEAD_SIZE = 128
QUERY_HEADS = 32
KEY_VALUE_HEADS = 4
TOK_DEV = 384
EDGE = 256
DOCS = 4

GROUP_HEADS = QUERY_HEADS // KEY_VALUE_HEADS
GROUP_COLS = GROUP_HEADS * HEAD_SIZE
KV_COLS = 2 * HEAD_SIZE
HEAD_ROWS = TOK_DEV - EDGE
WIDE = 256
ROWS = EDGE + TOK_DEV
ROWS_TOP = EDGE + HEAD_ROWS
SCALE = HEAD_SIZE**-0.5
LOG2E = math.log2(math.e)
MASKED = -1e30
VMEM_BYTES = 56 << 20
F32 = jnp.float32
BF16 = jnp.bfloat16
ANY = pl.BlockSpec(memory_space=pl.ANY)


def mul_nt(a, b):
    return lax.dot_general(a, b, (((1,), (1,)), ((), ())), preferred_element_type=F32)


def mul_nn(a, b):
    return lax.dot_general(a, b, (((1,), (0,)), ((), ())), preferred_element_type=F32)


def cols(head):
    return slice(head * HEAD_SIZE, (head + 1) * HEAD_SIZE)


def fill_bias(bias, first, second, third, edge_first):
    def doc(position):
        return (
            (position >= first).astype(jnp.int32)
            + (position >= second).astype(jnp.int32)
            + (position >= third).astype(jnp.int32)
        )

    key = lax.broadcasted_iota(jnp.int32, (EDGE, TOK_DEV), 0) + HEAD_ROWS
    query = lax.broadcasted_iota(jnp.int32, (EDGE, TOK_DEV), 1)
    bias[0:EDGE] = jnp.where((key >= edge_first) & (query < first), 0.0, MASKED)
    key = lax.broadcasted_iota(jnp.int32, (TOK_DEV, TOK_DEV), 0)
    query = lax.broadcasted_iota(jnp.int32, (TOK_DEV, TOK_DEV), 1)
    bias[EDGE:ROWS] = jnp.where((doc(key) == doc(query)) & (key <= query), 0.0, MASKED)


def group_kernel(aliased, me_ref, starts_ref, partner_ref, *refs):
    q_ref, g_ref, l_ref, d_ref, edge_k_ref, edge_v_ref, k_ref, v_ref = refs[:8]
    refs = refs[8 + aliased :]
    dq_ref, edge_grad_ref, own_grad_ref, bias, keys_t, total, p_late, s_late, p_early, s_early = refs
    step = pl.program_id(0)
    late = slice(HEAD_ROWS, TOK_DEV)
    early = slice(0, HEAD_ROWS)

    @pl.when(step == 0)
    def _():
        me = me_ref[0]
        other = partner_ref[me]
        fill_bias(bias, starts_ref[1, me], starts_ref[2, me], starts_ref[3, me], starts_ref[3, other])
        keys_t[:, 0:EDGE] = edge_k_ref[...].T
        keys_t[:, EDGE:ROWS] = k_ref[...].T
        total[...] = jnp.zeros_like(total)

    keys = jnp.concatenate([edge_k_ref[...], k_ref[...]], 0)
    values = jnp.concatenate([edge_v_ref[...], v_ref[...]], 0)

    def tile(q, g, norm, delta, rows, spread, p_out, s_out, at):
        for low in range(0, rows, 128):
            span = slice(low, low + 128)
            s = mul_nt(keys[span], q)
            dp = mul_nt(values[span], g)
            p = jnp.exp2((s * (SCALE * LOG2E) - norm) + spread(span))
            p_out[span, at : at + WIDE] = p.astype(BF16)
            s_out[span, at : at + WIDE] = (p * (dp - delta)).astype(BF16)

    def pair(ref):
        return jnp.concatenate([ref[early, cols(0)], ref[early, cols(1)]], 0)

    def late_pair(ref):
        return jnp.concatenate([ref[late, cols(0)], ref[late, cols(1)]], 0)

    def pair_row(rows):
        return jnp.concatenate([rows[0][:, early], rows[1][:, early]], 1)

    def twice(x):
        return jnp.concatenate([x, x], 1)

    norms = [l_ref[pl.ds(2 * step + j, 1), :] * LOG2E for j in range(2)]
    deltas = [d_ref[pl.ds(2 * step + j, 1), :] for j in range(2)]
    for j in range(2):
        tile(
            q_ref[late, cols(j)],
            g_ref[late, cols(j)],
            norms[j][:, late],
            deltas[j][:, late],
            ROWS,
            lambda span: bias[span, late],
            p_late,
            s_late,
            j * WIDE,
        )
    tile(
        pair(q_ref),
        pair(g_ref),
        pair_row(norms),
        pair_row(deltas),
        ROWS_TOP,
        lambda span: twice(bias[span, early]),
        p_early,
        s_early,
        0,
    )
    for j in range(2):
        x = mul_nn(keys_t[...], s_late[:, j * WIDE : (j + 1) * WIDE])
        dq_ref[late, cols(j)] = (x.T * SCALE).astype(BF16)
    x = (mul_nn(keys_t[:, :ROWS_TOP], s_early[...]).T * SCALE).astype(BF16)
    dq_ref[early, cols(0)] = x[:HEAD_ROWS]
    dq_ref[early, cols(1)] = x[HEAD_ROWS:]
    for j, (one, two, ref) in enumerate(((s_late, s_early, q_ref), (p_late, p_early, g_ref))):
        total[:, cols(j)] += mul_nn(one[...], late_pair(ref))
        total[0:ROWS_TOP, cols(j)] += mul_nn(two[...], pair(ref))

    @pl.when(step == pl.num_programs(0) - 1)
    def _():
        for j, scale in enumerate((SCALE, 1.0)):
            edge_grad_ref[:, cols(j)] = (total[0:EDGE, cols(j)] * scale).astype(BF16)
            own_grad_ref[:, cols(j)] = total[EDGE:ROWS, cols(j)] * scale


def group_grads(scalars, q, g, norms, deltas, keyvals, edge, group, edge_grad, own_grad):
    pairs = GROUP_HEADS // 2
    pair_cols = pl.BlockSpec((TOK_DEV, 2 * HEAD_SIZE), lambda i, *_: (0, group * pairs + i))
    rows = pl.BlockSpec((GROUP_HEADS, TOK_DEV), lambda i, *_: (group, 0))
    at_group = lambda i, *_: (0, group)
    at_values = lambda i, *_: (0, KEY_VALUE_HEADS + group)
    in_specs = [
        pair_cols,
        pair_cols,
        rows,
        rows,
        pl.BlockSpec((EDGE, HEAD_SIZE), at_group),
        pl.BlockSpec((EDGE, HEAD_SIZE), at_values),
        pl.BlockSpec((TOK_DEV, HEAD_SIZE), at_group),
        pl.BlockSpec((TOK_DEV, HEAD_SIZE), at_values),
    ]
    operands = [q, g, norms, deltas, edge, edge, keyvals, keyvals]
    aliases = {}
    for output, buffer in ((1, edge_grad), (2, own_grad)):
        if buffer is not None:
            aliases[len(scalars) + len(operands)] = output
            operands.append(buffer)
            in_specs.append(ANY)
    flops = 2 * 5 * TOK_DEV * ROWS * HEAD_SIZE * GROUP_HEADS
    return pl.pallas_call(
        functools.partial(group_kernel, len(aliases)),
        grid_spec=pltpu.PrefetchScalarGridSpec(
            num_scalar_prefetch=3,
            grid=(pairs,),
            in_specs=in_specs,
            out_specs=[
                pl.BlockSpec((TOK_DEV, 2 * HEAD_SIZE), lambda i, *_: (0, i)),
                pl.BlockSpec((EDGE, KV_COLS), at_group),
                pl.BlockSpec((TOK_DEV, KV_COLS), at_group),
            ],
            scratch_shapes=[
                pltpu.VMEM((ROWS, TOK_DEV), F32),
                pltpu.VMEM((HEAD_SIZE, ROWS), BF16),
                pltpu.VMEM((ROWS, KV_COLS), F32),
                pltpu.VMEM((ROWS, 2 * WIDE), BF16),
                pltpu.VMEM((ROWS, 2 * WIDE), BF16),
                pltpu.VMEM((ROWS_TOP, WIDE), BF16),
                pltpu.VMEM((ROWS_TOP, WIDE), BF16),
            ],
        ),
        out_shape=[
            jax.ShapeDtypeStruct((TOK_DEV, GROUP_COLS), BF16),
            jax.ShapeDtypeStruct((EDGE, KEY_VALUE_HEADS * KV_COLS), BF16),
            jax.ShapeDtypeStruct((TOK_DEV, KEY_VALUE_HEADS * KV_COLS), F32),
        ],
        input_output_aliases=aliases,
        cost_estimate=pl.CostEstimate(flops=2 * flops, bytes_accessed=4 << 20, transcendentals=0),
        compiler_params=pltpu.CompilerParams(vmem_limit_bytes=VMEM_BYTES),
        name="group_grads",
    )(*scalars, *operands)


def join_kernel(own_ref, back_ref, out_ref):
    for group in range(KEY_VALUE_HEADS):
        for part in range(2):
            source = cols(2 * group + part)
            target = cols(part * KEY_VALUE_HEADS + group)
            arrived = back_ref[:, source].astype(F32)
            out_ref[0:HEAD_ROWS, target] = own_ref[0:HEAD_ROWS, source].astype(BF16)
            out_ref[HEAD_ROWS:TOK_DEV, target] = (own_ref[HEAD_ROWS:TOK_DEV, source] + arrived).astype(BF16)


def join_grads(own, back):
    return pl.pallas_call(
        join_kernel,
        out_shape=jax.ShapeDtypeStruct((TOK_DEV, 2 * KEY_VALUE_HEADS * HEAD_SIZE), BF16),
        compiler_params=pltpu.CompilerParams(vmem_limit_bytes=VMEM_BYTES),
        name="join_grads",
    )(own, back)


def place_kernel(slot, *refs):
    chunk_ref, out_ref, done = refs[-3:]
    width = chunk_ref.shape[1]
    copy = pltpu.make_async_copy(chunk_ref, out_ref.at[0, :, slot * width : (slot + 1) * width], done)
    copy.start()
    copy.wait()


def place(total, chunk, slot, slots):
    operands = [chunk] if total is None else [total, chunk]
    return pl.pallas_call(
        functools.partial(place_kernel, slot),
        in_specs=[ANY] * len(operands),
        out_specs=ANY,
        out_shape=jax.ShapeDtypeStruct((1, chunk.shape[0], slots * chunk.shape[1]), chunk.dtype),
        input_output_aliases={} if total is None else {0: 0},
        scratch_shapes=[pltpu.SemaphoreType.DMA],
        compiler_params=pltpu.CompilerParams(vmem_limit_bytes=1 << 20),
        name="place",
    )(*operands)


def local(q_heads, key_value_heads, grad_out, log_norm, row_delta, doc_starts, partner):
    queries, outgrads, keyvals = q_heads[0], grad_out[0], key_value_heads[0]
    norms, deltas = log_norm[0], row_delta[0]
    ctx = lax.axis_size("ctx")
    pipe = lax.axis_size("pipe")
    bits = ctx.bit_length() - 1
    me = lax.axis_index("ctx")
    flipped = jnp.bitwise_xor(partner[0, me], me)
    digit = sum((flipped >= 1 << bit).astype(jnp.int32) for bit in range(1, bits))
    scalars = (me.astype(jnp.int32)[None], doc_starts[0].T, partner[0])

    def with_partner(block):
        def branch(bit):
            return lambda value: lax.ppermute(value, "ctx", [(low, low ^ 1 << bit) for low in range(ctx)])

        return lax.switch(digit, [branch(bit) for bit in range(bits)], block)

    def to_previous(chunk):
        return lax.ppermute(chunk, "pipe", [(source, (source - 1) % pipe) for source in range(pipe)])

    edge = with_partner(keyvals[HEAD_ROWS:])
    edge_grad = own_grad = None
    sent = []
    for group in range(KEY_VALUE_HEADS):
        dq, edge_grad, own_grad = group_grads(
            scalars, queries, outgrads, norms, deltas, keyvals, edge, group, edge_grad, own_grad
        )
        sent.append(to_previous(dq))
    back = with_partner(edge_grad)
    sent.append(to_previous(join_grads(own_grad, back)))
    total = None
    for slot, chunk in enumerate(sent):
        total = place(total, chunk, slot, len(sent))
    return total


def solution(mesh):
    in_specs = (
        P("pipe", "ctx", None),
        P("pipe", "ctx", None),
        P("pipe", "ctx", None),
        P("pipe", None, "ctx"),
        P("pipe", None, "ctx"),
        P("pipe", None, None),
        P("pipe", None),
    )
    out_specs = P("pipe", "ctx", None)
    return jax.shard_map(local, mesh=mesh, in_specs=in_specs, out_specs=out_specs, check_vma=False)
```

```python
import functools
import math

import jax
import jax.numpy as jnp
from jax import lax
from jax.experimental import pallas as pl
from jax.experimental.pallas import tpu as pltpu
from jax.sharding import PartitionSpec as P

HEAD_SIZE = 128
QUERY_HEADS = 32
KEY_VALUE_HEADS = 4
TOK_DEV = 384
EDGE = 256
DOCS = 4

GROUP_HEADS = QUERY_HEADS // KEY_VALUE_HEADS
GROUP_COLS = GROUP_HEADS * HEAD_SIZE
KV_COLS = 2 * HEAD_SIZE
HEAD_ROWS = TOK_DEV - EDGE
WIDE = 256
ROWS = EDGE + TOK_DEV
ROWS_TOP = EDGE + HEAD_ROWS
FOLDS = GROUP_HEADS // 2
FOLD_ROWS = HEAD_ROWS // FOLDS
CHUNK_ROWS = TOK_DEV + FOLD_ROWS
DIGITS = 6
SCALE = HEAD_SIZE**-0.5
LOG2E = math.log2(math.e)
MASKED = -1e30
VMEM_BYTES = 56 << 20
F32 = jnp.float32
BF16 = jnp.bfloat16
ANY = pl.BlockSpec(memory_space=pl.ANY)


def mul_nt(a, b):
    return lax.dot_general(a, b, (((1,), (1,)), ((), ())), preferred_element_type=F32)


def mul_nn(a, b):
    return lax.dot_general(a, b, (((1,), (0,)), ((), ())), preferred_element_type=F32)


def cols(head):
    return slice(head * HEAD_SIZE, (head + 1) * HEAD_SIZE)


def prepare_kernel(me_ref, starts_ref, partner_ref, top_ref, bottom_ref, digit_ref, info_ref, *edge_refs):
    me = me_ref[0]
    other = partner_ref[0, me]
    flipped = jnp.bitwise_xor(me, other)
    digit = jnp.int32(0)
    for bit in range(1, DIGITS):
        digit += jnp.where(flipped >= 1 << bit, 1, 0)
    digit_ref[0] = digit
    for piece in range(1, DOCS):
        info_ref[piece] = starts_ref[piece, me]
    info_ref[0] = starts_ref[DOCS - 1, other]
    for group, edge_ref in enumerate(edge_refs):
        for part in range(2):
            source = cols(part * KEY_VALUE_HEADS + group)
            edge_ref[0:HEAD_ROWS, cols(part)] = top_ref[:, source]
            edge_ref[HEAD_ROWS:EDGE, cols(part)] = bottom_ref[:, source]


def prepare(me, starts, partner, keyvals):
    smem = pl.BlockSpec(memory_space=pltpu.SMEM)
    rows = lambda at: pl.BlockSpec((HEAD_ROWS, keyvals.shape[1]), lambda i: (at, 0))
    edge = pl.BlockSpec((EDGE, KV_COLS), lambda i: (0, 0))
    return pl.pallas_call(
        prepare_kernel,
        grid=(1,),
        in_specs=[smem] * 3 + [rows(1), rows(2)],
        out_specs=[smem] * 2 + [edge] * KEY_VALUE_HEADS,
        out_shape=[jax.ShapeDtypeStruct((1,), jnp.int32), jax.ShapeDtypeStruct((DOCS,), jnp.int32)]
        + [jax.ShapeDtypeStruct((EDGE, KV_COLS), BF16)] * KEY_VALUE_HEADS,
        compiler_params=pltpu.CompilerParams(vmem_limit_bytes=VMEM_BYTES),
        name="prepare",
    )(me, starts, partner, keyvals, keyvals)


def fill_bias(bias, info_ref):
    def doc(position):
        return sum((position >= info_ref[piece]).astype(jnp.int32) for piece in range(1, DOCS))

    key = lax.broadcasted_iota(jnp.int32, (EDGE, 1), 0) + HEAD_ROWS
    query = lax.broadcasted_iota(jnp.int32, (1, TOK_DEV), 1)
    bias[0:EDGE] = jnp.where((key >= info_ref[0]) & (query < info_ref[1]), 0.0, MASKED)
    key = lax.broadcasted_iota(jnp.int32, (TOK_DEV, 1), 0)
    bias[EDGE:ROWS] = jnp.where((doc(key) == doc(query)) & (key <= query), 0.0, MASKED)


def grads_of(keys, values, q, g, norm, delta, bias):
    s = mul_nt(keys, q)
    dp = mul_nt(values, g)
    p = jnp.exp2((s * (SCALE * LOG2E) - norm) + bias)
    return p.astype(BF16), (p * (dp - delta)).astype(BF16)


def twice(x):
    return jnp.concatenate([x, x], 1)


EARLY = slice(0, HEAD_ROWS)
LATE = slice(HEAD_ROWS, TOK_DEV)


def group_kernel(*refs):
    info_ref, q_ref, g_ref, l_ref, d_ref, edge_k_ref, edge_v_ref, k_ref, v_ref = refs[:9]
    out_ref, swap_ref, late_grad_ref, bias, keys_t, total, p_late, s_late, p_early, s_early = refs[-10:]
    step = pl.program_id(0)
    out_cols = [pl.ds(pl.multiple_of((2 * step + j) * HEAD_SIZE, HEAD_SIZE), HEAD_SIZE) for j in range(2)]

    @pl.when(step == 0)
    def _():
        fill_bias(bias, info_ref)
        keys_t[:, 0:EDGE] = edge_k_ref[...].T
        keys_t[:, EDGE:ROWS] = k_ref[...].T
        total[...] = jnp.zeros_like(total)

    keys = jnp.concatenate([edge_k_ref[...], k_ref[...]], 0)
    values = jnp.concatenate([edge_v_ref[...], v_ref[...]], 0)

    def pair(ref, span):
        return jnp.concatenate([ref[span, cols(0)], ref[span, cols(1)]], 0)

    def pair_row(rows, span):
        return jnp.concatenate([rows[0][:, span], rows[1][:, span]], 1)

    norms = [l_ref[pl.ds(2 * step + j, 1), :] * LOG2E for j in range(2)]
    deltas = [d_ref[pl.ds(2 * step + j, 1), :] for j in range(2)]
    for j in range(2):
        q = q_ref[LATE, cols(j)]
        g = g_ref[LATE, cols(j)]
        columns = slice(j * WIDE, (j + 1) * WIDE)
        for low in range(0, ROWS, 128):
            span = slice(low, low + 128)
            p_late[span, columns], s_late[span, columns] = grads_of(
                keys[span], values[span], q, g, norms[j][:, LATE], deltas[j][:, LATE], bias[span, LATE]
            )
    q = pair(q_ref, EARLY)
    g = pair(g_ref, EARLY)
    for low in range(0, ROWS_TOP, 128):
        span = slice(low, low + 128)
        p_early[span], s_early[span] = grads_of(
            keys[span], values[span], q, g, pair_row(norms, EARLY), pair_row(deltas, EARLY), twice(bias[span, EARLY])
        )
    for j in range(2):
        x = mul_nn(keys_t[...], s_late[:, j * WIDE : (j + 1) * WIDE])
        out_ref[LATE, out_cols[j]] = (x.T * SCALE).astype(BF16)
    x = (mul_nn(keys_t[:, :ROWS_TOP], s_early[...]).T * SCALE).astype(BF16)
    out_ref[EARLY, out_cols[0]] = x[:HEAD_ROWS]
    out_ref[EARLY, out_cols[1]] = x[HEAD_ROWS:]
    for j, (late, early, ref) in enumerate(((s_late, s_early, q_ref), (p_late, p_early, g_ref))):
        total[:, cols(j)] += mul_nn(late[...], pair(ref, LATE))
        total[0:ROWS_TOP, cols(j)] += mul_nn(early[...], pair(ref, EARLY))

    @pl.when(step == pl.num_programs(0) - 1)
    def _():
        fresh = swap_ref.shape[0] - EDGE
        if fresh:
            swap_ref[0:fresh] = refs[9][...]
        for j, scale in enumerate((SCALE, 1.0)):
            swap_ref[fresh:, cols(j)] = (total[0:EDGE, cols(j)] * scale).astype(BF16)
            early = (total[EDGE:ROWS_TOP, cols(j)] * scale).astype(BF16)
            for at in range(FOLDS):
                out_ref[TOK_DEV:CHUNK_ROWS, cols(j * FOLDS + at)] = early[at * FOLD_ROWS : (at + 1) * FOLD_ROWS]
            late_grad_ref[:, cols(j)] = total[ROWS_TOP:ROWS, cols(j)] * scale


def group_grads(group, info, q, g, norms, deltas, keyvals, edge, *next_rows):
    pairs = GROUP_HEADS // 2
    pair_cols = pl.BlockSpec((TOK_DEV, 2 * HEAD_SIZE), lambda i: (0, group * pairs + i))
    rows = pl.BlockSpec((GROUP_HEADS, TOK_DEV), lambda i: (group, 0))
    at_group = lambda i: (0, group)
    at_values = lambda i: (0, KEY_VALUE_HEADS + group)
    in_specs = [
        pl.BlockSpec(memory_space=pltpu.SMEM),
        pair_cols,
        pair_cols,
        rows,
        rows,
        pl.BlockSpec((EDGE, HEAD_SIZE), lambda i: (0, 0)),
        pl.BlockSpec((EDGE, HEAD_SIZE), lambda i: (0, 1)),
        pl.BlockSpec((TOK_DEV, HEAD_SIZE), at_group),
        pl.BlockSpec((TOK_DEV, HEAD_SIZE), at_values),
    ]
    operands = [info, q, g, norms, deltas, edge, edge, keyvals, keyvals, *next_rows]
    flops = 2 * 5 * TOK_DEV * ROWS * HEAD_SIZE * GROUP_HEADS
    whole = lambda *shape: pl.BlockSpec(shape, lambda i: (0, 0))
    in_specs += [whole(EDGE, KV_COLS)] * len(next_rows)
    swap_rows = EDGE * (1 + len(next_rows))
    return pl.pallas_call(
        group_kernel,
        grid=(pairs,),
        in_specs=in_specs,
        out_specs=[
            whole(CHUNK_ROWS, GROUP_COLS),
            whole(swap_rows, KV_COLS),
            whole(EDGE, KV_COLS),
        ],
        scratch_shapes=[
            pltpu.VMEM((ROWS, TOK_DEV), F32),
            pltpu.VMEM((HEAD_SIZE, ROWS), BF16),
            pltpu.VMEM((ROWS, KV_COLS), F32),
            pltpu.VMEM((ROWS, 2 * WIDE), BF16),
            pltpu.VMEM((ROWS, 2 * WIDE), BF16),
            pltpu.VMEM((ROWS_TOP, WIDE), BF16),
            pltpu.VMEM((ROWS_TOP, WIDE), BF16),
        ],
        out_shape=[
            jax.ShapeDtypeStruct((CHUNK_ROWS, GROUP_COLS), BF16),
            jax.ShapeDtypeStruct((swap_rows, KV_COLS), BF16),
            jax.ShapeDtypeStruct((EDGE, KV_COLS), F32),
        ],
        cost_estimate=pl.CostEstimate(flops=2 * flops, bytes_accessed=4 << 20, transcendentals=0),
        compiler_params=pltpu.CompilerParams(vmem_limit_bytes=VMEM_BYTES),
        name="group_grads",
    )(*operands)


def join_kernel(*refs):
    out_ref = refs[-1]
    for at in range(len(refs) // 2):
        own_ref, back_ref = refs[2 * at : 2 * at + 2]
        out_ref[:, at * KV_COLS : (at + 1) * KV_COLS] = (own_ref[...] + back_ref[back_ref.shape[0] - EDGE :].astype(F32)).astype(BF16)


def join_grads(pairs):
    return pl.pallas_call(
        join_kernel,
        out_shape=jax.ShapeDtypeStruct((EDGE, len(pairs) * KV_COLS), BF16),
        compiler_params=pltpu.CompilerParams(vmem_limit_bytes=6 << 20),
        name="join_grads",
    )(*[block for pair in pairs for block in pair])


def place_kernel(pieces, *refs):
    chunk_ref, out_ref, done = refs[-3:]
    copies = [
        pltpu.make_async_copy(chunk_ref.at[source], out_ref.at[0, *target], done.at[at])
        for at, (source, target) in enumerate(pieces)
    ]
    for copy in copies:
        copy.start()
    for copy in copies:
        copy.wait()


def place(total, chunk, pieces):
    operands = [chunk] if total is None else [total, chunk]
    vmem = pl.BlockSpec(memory_space=pltpu.VMEM)
    width = QUERY_HEADS * HEAD_SIZE + KEY_VALUE_HEADS * KV_COLS
    return pl.pallas_call(
        functools.partial(place_kernel, pieces),
        in_specs=[vmem] if total is None else [ANY, vmem],
        out_specs=ANY,
        out_shape=jax.ShapeDtypeStruct((1, TOK_DEV, width), chunk.dtype),
        input_output_aliases={} if total is None else {0: 0},
        scratch_shapes=[pltpu.SemaphoreType.DMA((len(pieces),))],
        compiler_params=pltpu.CompilerParams(vmem_limit_bytes=4 << 20),
        name="place",
    )(*operands)


def keyval_cols(part, group):
    return cols(QUERY_HEADS + part * KEY_VALUE_HEADS + group)


def place_chunk(total, chunk, group):
    rows = slice(0, TOK_DEV)
    pieces = [((rows, slice(0, GROUP_COLS)), (rows, slice(group * GROUP_COLS, (group + 1) * GROUP_COLS)))]
    for part in range(2):
        for at in range(FOLDS):
            source = (slice(TOK_DEV, CHUNK_ROWS), cols(part * FOLDS + at))
            pieces.append((source, (slice(at * FOLD_ROWS, (at + 1) * FOLD_ROWS), keyval_cols(part, group))))
    return place(total, chunk, pieces)


def place_late(total, chunk, groups):
    pieces = []
    for at, group in enumerate(groups):
        for part in range(2):
            pieces.append(((slice(0, EDGE), cols(2 * at + part)), (LATE, keyval_cols(part, group))))
    return place(total, chunk, pieces)


def local(q_heads, key_value_heads, grad_out, log_norm, row_delta, doc_starts, partner):
    queries, outgrads, keyvals = q_heads[0], grad_out[0], key_value_heads[0]
    norms, deltas = log_norm[0], row_delta[0]
    ctx = lax.axis_size("ctx")
    assert ctx == 1 << DIGITS
    pipe = lax.axis_size("pipe")
    me = lax.axis_index("ctx").astype(jnp.int32)[None]
    digit, info, *edge_rows = prepare(me, doc_starts[0].T, partner, keyvals)

    def stage(rows, *work):
        def branch(bit):
            def run(rows, *operands):
                arrived = lax.ppermute(rows, "ctx", [(low, low ^ 1 << bit) for low in range(ctx)])
                return arrived, group_grads(work[0], *operands) if work else []

            return run

        return lax.switch(digit[0], [branch(bit) for bit in range(DIGITS)], rows, *work[1:])

    def to_previous(chunk):
        return lax.ppermute(chunk, "pipe", [(source, (source - 1) % pipe) for source in range(pipe)])

    last = KEY_VALUE_HEADS - 1
    common = (info, queries, outgrads, norms, deltas, keyvals)
    arrived, _ = stage(edge_rows[0])
    swap = edge_rows[1]
    sent, owns, backs = [], [], []
    for group in range(KEY_VALUE_HEADS):
        edge = arrived
        arrived, (chunk, swap, own) = stage(swap, group, *common, edge, *edge_rows[group + 2 : group + 3])
        sent.append(to_previous(chunk))
        owns.append(own)
        backs.append(arrived)
    most = join_grads(list(zip(owns[:last], backs[1:])))
    most, swap = lax.optimization_barrier((most, swap))
    most = to_previous(most)
    arrived, _ = stage(swap)
    rest = to_previous(join_grads([(owns[last], arrived)]))
    total = None
    for group, chunk in enumerate(sent):
        total = place_chunk(total, chunk, group)
    total = place_late(total, most, range(last))
    return place_late(total, rest, [last])


def solution(mesh):
    in_specs = (
        P("pipe", "ctx", None),
        P("pipe", "ctx", None),
        P("pipe", "ctx", None),
        P("pipe", None, "ctx"),
        P("pipe", None, "ctx"),
        P("pipe", None, None),
        P("pipe", None),
    )
    out_specs = P("pipe", "ctx", None)
    return jax.shard_map(local, mesh=mesh, in_specs=in_specs, out_specs=out_specs, check_vma=False)
```

```python
import functools
import math

import jax
import jax.numpy as jnp
from jax import lax
from jax.experimental import pallas as pl
from jax.experimental.pallas import tpu as pltpu
from jax.sharding import PartitionSpec as P

HEAD_SIZE = 128
QUERY_HEADS = 32
KEY_VALUE_HEADS = 4
TOK_DEV = 384
EDGE = 256
DOCS = 4

GROUP_HEADS = QUERY_HEADS // KEY_VALUE_HEADS
GROUP_COLS = GROUP_HEADS * HEAD_SIZE
KV_COLS = 2 * HEAD_SIZE
HEAD_ROWS = TOK_DEV - EDGE
WIDE = 256
ROWS = EDGE + TOK_DEV
ROWS_TOP = EDGE + HEAD_ROWS
PAIRS = GROUP_HEADS // 2
FOLDS = 4
FOLD_ROWS = HEAD_ROWS // FOLDS
CHUNK_ROWS = TOK_DEV + FOLD_ROWS
DIGITS = 6
SCALE = HEAD_SIZE**-0.5
LOG2E = math.log2(math.e)
MASKED = -1e30
VMEM_BYTES = 56 << 20
F32 = jnp.float32
BF16 = jnp.bfloat16
ANY = pl.BlockSpec(memory_space=pl.ANY)


def mul_nt(a, b):
    return lax.dot_general(a, b, (((1,), (1,)), ((), ())), preferred_element_type=F32)


def mul_nn(a, b):
    return lax.dot_general(a, b, (((1,), (0,)), ((), ())), preferred_element_type=F32)


def cols(head):
    return slice(head * HEAD_SIZE, (head + 1) * HEAD_SIZE)


def prepare_kernel(me_ref, starts_ref, partner_ref, top_ref, bottom_ref, digit_ref, info_ref, *edge_refs):
    me = me_ref[0]
    other = partner_ref[0, me]
    flipped = jnp.bitwise_xor(me, other)
    digit = jnp.int32(0)
    for bit in range(1, DIGITS):
        digit += jnp.where(flipped >= 1 << bit, 1, 0)
    digit_ref[0] = digit
    for piece in range(1, DOCS):
        info_ref[piece] = starts_ref[piece, me]
    info_ref[0] = starts_ref[DOCS - 1, other]
    for group in range(KEY_VALUE_HEADS):
        edge_ref = edge_refs[min(group, 1)]
        for part in range(2):
            source = cols(part * KEY_VALUE_HEADS + group)
            target = cols(2 * max(group - 1, 0) + part)
            edge_ref[0:HEAD_ROWS, target] = top_ref[:, source]
            edge_ref[HEAD_ROWS:EDGE, target] = bottom_ref[:, source]


def prepare(me, starts, partner, keyvals):
    smem = pl.BlockSpec(memory_space=pltpu.SMEM)
    rows = lambda at: pl.BlockSpec((HEAD_ROWS, keyvals.shape[1]), lambda i: (at, 0))
    edges = [(EDGE, KV_COLS), (EDGE, (KEY_VALUE_HEADS - 1) * KV_COLS)]
    return pl.pallas_call(
        prepare_kernel,
        grid=(1,),
        in_specs=[smem] * 3 + [rows(1), rows(2)],
        out_specs=[smem] * 2 + [pl.BlockSpec(shape, lambda i: (0, 0)) for shape in edges],
        out_shape=[jax.ShapeDtypeStruct((1,), jnp.int32), jax.ShapeDtypeStruct((DOCS,), jnp.int32)]
        + [jax.ShapeDtypeStruct(shape, BF16) for shape in edges],
        compiler_params=pltpu.CompilerParams(vmem_limit_bytes=VMEM_BYTES),
        name="prepare",
    )(me, starts, partner, keyvals, keyvals)


def fill_bias(bias, info_ref):
    def doc(position):
        return sum((position >= info_ref[piece]).astype(jnp.int32) for piece in range(1, DOCS))

    key = lax.broadcasted_iota(jnp.int32, (EDGE, 1), 0) + HEAD_ROWS
    query = lax.broadcasted_iota(jnp.int32, (1, TOK_DEV), 1)
    bias[0:EDGE] = jnp.where((key >= info_ref[0]) & (query < info_ref[1]), 0.0, MASKED)
    key = lax.broadcasted_iota(jnp.int32, (TOK_DEV, 1), 0)
    bias[EDGE:ROWS] = jnp.where((doc(key) == doc(query)) & (key <= query), 0.0, MASKED)


def grads_of(keys, values, q, g, norm, delta, bias):
    s = mul_nt(keys, q)
    dp = mul_nt(values, g)
    p = jnp.exp2((s * (SCALE * LOG2E) - norm) + bias)
    return p.astype(BF16), (p * (dp - delta)).astype(BF16)


def twice(x):
    return jnp.concatenate([x, x], 1)


EARLY = slice(0, HEAD_ROWS)
LATE = slice(HEAD_ROWS, TOK_DEV)


def group_kernel(older, *refs):
    info_ref, q_ref, g_ref, l_ref, d_ref, edge_k_ref, edge_v_ref, k_ref, v_ref = refs[:9]
    out_ref, swap_ref, late_grad_ref, bias, keys_t, total, p_late, s_late, p_early, s_early = refs[-10:]
    step = pl.program_id(0)
    place = lax.rem(step, PAIRS)
    out_cols = [pl.ds(pl.multiple_of((2 * place + j) * HEAD_SIZE, HEAD_SIZE), HEAD_SIZE) for j in range(2)]

    @pl.when(step == 0)
    def _():
        fill_bias(bias, info_ref)
        if older:
            swap_ref[:, 0 : older * KV_COLS] = refs[9][...]

    @pl.when(place == 0)
    def _():
        keys_t[:, 0:EDGE] = edge_k_ref[...].T
        keys_t[:, EDGE:ROWS] = k_ref[...].T
        total[...] = jnp.zeros_like(total)

    keys = jnp.concatenate([edge_k_ref[...], k_ref[...]], 0)
    values = jnp.concatenate([edge_v_ref[...], v_ref[...]], 0)

    def pair(ref, span):
        return jnp.concatenate([ref[span, cols(0)], ref[span, cols(1)]], 0)

    def pair_row(rows, span):
        return jnp.concatenate([rows[0][:, span], rows[1][:, span]], 1)

    norms = [l_ref[pl.ds(2 * place + j, 1), :] * LOG2E for j in range(2)]
    deltas = [d_ref[pl.ds(2 * place + j, 1), :] for j in range(2)]
    for j in range(2):
        q = q_ref[LATE, cols(j)]
        g = g_ref[LATE, cols(j)]
        columns = slice(j * WIDE, (j + 1) * WIDE)
        for low in range(0, ROWS, 128):
            span = slice(low, low + 128)
            p_late[span, columns], s_late[span, columns] = grads_of(
                keys[span], values[span], q, g, norms[j][:, LATE], deltas[j][:, LATE], bias[span, LATE]
            )
    q = pair(q_ref, EARLY)
    g = pair(g_ref, EARLY)
    for low in range(0, ROWS_TOP, 128):
        span = slice(low, low + 128)
        p_early[span], s_early[span] = grads_of(
            keys[span], values[span], q, g, pair_row(norms, EARLY), pair_row(deltas, EARLY), twice(bias[span, EARLY])
        )
    for j in range(2):
        x = mul_nn(keys_t[...], s_late[:, j * WIDE : (j + 1) * WIDE])
        out_ref[LATE, out_cols[j]] = (x.T * SCALE).astype(BF16)
    x = (mul_nn(keys_t[:, :ROWS_TOP], s_early[...]).T * SCALE).astype(BF16)
    out_ref[EARLY, out_cols[0]] = x[:HEAD_ROWS]
    out_ref[EARLY, out_cols[1]] = x[HEAD_ROWS:]
    for j, (late, early, ref) in enumerate(((s_late, s_early, q_ref), (p_late, p_early, g_ref))):
        total[:, cols(j)] += mul_nn(late[...], pair(ref, LATE))
        total[0:ROWS_TOP, cols(j)] += mul_nn(early[...], pair(ref, EARLY))

    @pl.when(place == PAIRS - 1)
    def _():
        group = lax.div(step, PAIRS) + older
        for j, scale in enumerate((SCALE, 1.0)):
            to_swap = pl.ds(pl.multiple_of(group * KV_COLS + j * HEAD_SIZE, HEAD_SIZE), HEAD_SIZE)
            swap_ref[:, to_swap] = (total[0:EDGE, cols(j)] * scale).astype(BF16)
            early = (total[EDGE:ROWS_TOP, cols(j)] * scale).astype(BF16)
            for at in range(FOLDS):
                out_ref[TOK_DEV:CHUNK_ROWS, cols(j * FOLDS + at)] = early[at * FOLD_ROWS : (at + 1) * FOLD_ROWS]
            late_grad_ref[:, cols(j)] = total[ROWS_TOP:ROWS, cols(j)] * scale


def group_grads(first, count, edge_at, info, q, g, norms, deltas, keyvals, edge, *older):
    group_of = lambda i: first + i // PAIRS
    pair_cols = pl.BlockSpec((TOK_DEV, 2 * HEAD_SIZE), lambda i: (0, first * PAIRS + i))
    rows = pl.BlockSpec((GROUP_HEADS, TOK_DEV), lambda i: (group_of(i), 0))
    part = lambda height, at: pl.BlockSpec((height, HEAD_SIZE), lambda i: (0, at(group_of(i))))
    whole = lambda *shape: pl.BlockSpec(shape, lambda i: (0, 0))
    in_specs = [
        pl.BlockSpec(memory_space=pltpu.SMEM),
        pair_cols,
        pair_cols,
        rows,
        rows,
        part(EDGE, lambda group: 2 * (group - edge_at)),
        part(EDGE, lambda group: 2 * (group - edge_at) + 1),
        part(TOK_DEV, lambda group: group),
        part(TOK_DEV, lambda group: KEY_VALUE_HEADS + group),
    ]
    operands = [info, q, g, norms, deltas, edge, edge, keyvals, keyvals, *older]
    in_specs += [whole(*block.shape) for block in older]
    earlier = sum(block.shape[1] for block in older) // KV_COLS
    swap = (EDGE, (earlier + count) * KV_COLS)
    return pl.pallas_call(
        functools.partial(group_kernel, earlier),
        grid=(count * PAIRS,),
        in_specs=in_specs,
        out_specs=[
            pl.BlockSpec((CHUNK_ROWS, GROUP_COLS), lambda i: (i // PAIRS, 0)),
            whole(*swap),
            pl.BlockSpec((EDGE, KV_COLS), lambda i: (0, i // PAIRS)),
        ],
        scratch_shapes=[
            pltpu.VMEM((ROWS, TOK_DEV), F32),
            pltpu.VMEM((HEAD_SIZE, ROWS), BF16),
            pltpu.VMEM((ROWS, KV_COLS), F32),
            pltpu.VMEM((ROWS, 2 * WIDE), BF16),
            pltpu.VMEM((ROWS, 2 * WIDE), BF16),
            pltpu.VMEM((ROWS_TOP, WIDE), BF16),
            pltpu.VMEM((ROWS_TOP, WIDE), BF16),
        ],
        out_shape=[
            jax.ShapeDtypeStruct((count * CHUNK_ROWS, GROUP_COLS), BF16),
            jax.ShapeDtypeStruct(swap, BF16),
            jax.ShapeDtypeStruct((EDGE, count * KV_COLS), F32),
        ],
        cost_estimate=pl.CostEstimate(flops=1 << 20, bytes_accessed=1 << 16, transcendentals=0),
        compiler_params=pltpu.CompilerParams(vmem_limit_bytes=VMEM_BYTES),
        name="group_grads",
    )(*operands)


def join_kernel(*refs):
    *own_refs, back_ref, out_ref = refs
    at = 0
    for own_ref in own_refs:
        columns = slice(at, at + own_ref.shape[1])
        out_ref[:, columns] = (own_ref[...] + back_ref[:, columns].astype(F32)).astype(BF16)
        at += own_ref.shape[1]


def join_grads(owns, back):
    return pl.pallas_call(
        join_kernel,
        out_shape=jax.ShapeDtypeStruct(back.shape, BF16),
        compiler_params=pltpu.CompilerParams(vmem_limit_bytes=VMEM_BYTES),
        name="join_grads",
    )(*owns, back)


def place_kernel(pieces, *refs):
    chunk_ref, out_ref, done = refs[-3:]
    copies = [
        pltpu.make_async_copy(chunk_ref.at[source], out_ref.at[0, *target], done.at[at])
        for at, (source, target) in enumerate(pieces)
    ]
    for copy in copies:
        copy.start()
    for copy in copies:
        copy.wait()


def place(total, chunk, pieces):
    operands = [chunk] if total is None else [total, chunk]
    vmem = pl.BlockSpec(memory_space=pltpu.VMEM)
    width = QUERY_HEADS * HEAD_SIZE + KEY_VALUE_HEADS * KV_COLS
    return pl.pallas_call(
        functools.partial(place_kernel, pieces),
        in_specs=[vmem] if total is None else [ANY, vmem],
        out_specs=ANY,
        out_shape=jax.ShapeDtypeStruct((1, TOK_DEV, width), chunk.dtype),
        input_output_aliases={} if total is None else {0: 0},
        scratch_shapes=[pltpu.SemaphoreType.DMA((len(pieces),))],
        compiler_params=pltpu.CompilerParams(vmem_limit_bytes=4 << 20),
        name="place",
    )(*operands)


def keyval_cols(part, group):
    return cols(QUERY_HEADS + part * KEY_VALUE_HEADS + group)


def place_chunk(total, chunk, first):
    pieces = []
    for row in range(0, chunk.shape[0], CHUNK_ROWS):
        group = first + row // CHUNK_ROWS
        rows = slice(0, TOK_DEV)
        pieces.append(
            (
                (slice(row, row + TOK_DEV), slice(0, GROUP_COLS)),
                (rows, slice(group * GROUP_COLS, (group + 1) * GROUP_COLS)),
            )
        )
        for part in range(2):
            for at in range(FOLDS):
                source = (slice(row + TOK_DEV, row + CHUNK_ROWS), cols(part * FOLDS + at))
                pieces.append((source, (slice(at * FOLD_ROWS, (at + 1) * FOLD_ROWS), keyval_cols(part, group))))
    return place(total, chunk, pieces)


def place_late(total, chunk, groups):
    pieces = []
    for at, group in enumerate(groups):
        for part in range(2):
            pieces.append(((slice(0, EDGE), cols(2 * at + part)), (LATE, keyval_cols(part, group))))
    return place(total, chunk, pieces)


def local(q_heads, key_value_heads, grad_out, log_norm, row_delta, doc_starts, partner):
    queries, outgrads, keyvals = q_heads[0], grad_out[0], key_value_heads[0]
    norms, deltas = log_norm[0], row_delta[0]
    ctx = lax.axis_size("ctx")
    assert ctx == 1 << DIGITS
    pipe = lax.axis_size("pipe")
    me = lax.axis_index("ctx").astype(jnp.int32)[None]
    digit, info, first_rows, other_rows = prepare(me, doc_starts[0].T, partner, keyvals)

    def stage(rows, work=None, *operands):
        def branch(bit):
            def run(rows, *operands):
                arrived = lax.ppermute(rows, "ctx", [(low, low ^ 1 << bit) for low in range(ctx)])
                return arrived, group_grads(*work, *operands) if work else []

            return run

        return lax.switch(digit[0], [branch(bit) for bit in range(DIGITS)], rows, *operands)

    def to_previous(chunk):
        return lax.ppermute(chunk, "pipe", [(source, (source - 1) % pipe) for source in range(pipe)])

    common = (info, queries, outgrads, norms, deltas, keyvals)
    edge, _ = stage(first_rows)
    edges, (chunk, swap, own) = stage(other_rows, (0, 1, 0), *common, edge)
    sent, owns = [(0, to_previous(chunk))], [own]
    for first, count in ((1, 1), (2, 2)):
        chunk, swap, own = group_grads(first, count, 1, *common, edges, swap)
        sent.append((first, to_previous(chunk)))
        owns.append(own)
    back, _ = stage(swap)
    late_grad = to_previous(join_grads(owns, back))
    total = None
    for first, chunk in sent:
        total = place_chunk(total, chunk, first)
    return place_late(total, late_grad, range(KEY_VALUE_HEADS))


def solution(mesh):
    in_specs = (
        P("pipe", "ctx", None),
        P("pipe", "ctx", None),
        P("pipe", "ctx", None),
        P("pipe", None, "ctx"),
        P("pipe", None, "ctx"),
        P("pipe", None, None),
        P("pipe", None),
    )
    out_specs = P("pipe", "ctx", None)
    return jax.shard_map(local, mesh=mesh, in_specs=in_specs, out_specs=out_specs, check_vma=False)
```

```python
import functools
import math

import jax
import jax.numpy as jnp
from jax import lax
from jax.experimental import pallas as pl
from jax.experimental.pallas import tpu as pltpu
from jax.sharding import PartitionSpec as P

HEAD_SIZE = 128
QUERY_HEADS = 32
KEY_VALUE_HEADS = 4
TOK_DEV = 384
EDGE = 256
DOCS = 4

GROUP_HEADS = QUERY_HEADS // KEY_VALUE_HEADS
GROUP_COLS = GROUP_HEADS * HEAD_SIZE
KV_COLS = 2 * HEAD_SIZE
HEAD_ROWS = TOK_DEV - EDGE
WIDE = 256
ROWS = EDGE + TOK_DEV
ROWS_TOP = EDGE + HEAD_ROWS
PAIRS = GROUP_HEADS // 2
FOLDS = 4
FOLD_ROWS = HEAD_ROWS // FOLDS
CHUNK_ROWS = TOK_DEV + FOLD_ROWS
DIGITS = 6
SCALE = HEAD_SIZE**-0.5
LOG2E = math.log2(math.e)
MASKED = -1e30
VMEM_BYTES = 56 << 20
F32 = jnp.float32
BF16 = jnp.bfloat16
ANY = pl.BlockSpec(memory_space=pl.ANY)


def mul_nt(a, b):
    return lax.dot_general(a, b, (((1,), (1,)), ((), ())), preferred_element_type=F32)


def mul_nn(a, b):
    return lax.dot_general(a, b, (((1,), (0,)), ((), ())), preferred_element_type=F32)


def cols(head):
    return slice(head * HEAD_SIZE, (head + 1) * HEAD_SIZE)


def prepare_kernel(me_ref, starts_ref, partner_ref, top_ref, bottom_ref, digit_ref, info_ref, *edge_refs):
    me = me_ref[0]
    other = partner_ref[0, me]
    flipped = jnp.bitwise_xor(me, other)
    digit = jnp.int32(0)
    for bit in range(1, DIGITS):
        digit += jnp.where(flipped >= 1 << bit, 1, 0)
    digit_ref[0] = digit
    for piece in range(1, DOCS):
        info_ref[piece] = starts_ref[piece, me]
    info_ref[0] = starts_ref[DOCS - 1, other]
    for group in range(KEY_VALUE_HEADS):
        edge_ref = edge_refs[min(group, 1)]
        for part in range(2):
            source = cols(part * KEY_VALUE_HEADS + group)
            target = cols(2 * max(group - 1, 0) + part)
            edge_ref[0:HEAD_ROWS, target] = top_ref[:, source]
            edge_ref[HEAD_ROWS:EDGE, target] = bottom_ref[:, source]


def prepare(me, starts, partner, keyvals):
    smem = pl.BlockSpec(memory_space=pltpu.SMEM)
    rows = lambda at: pl.BlockSpec((HEAD_ROWS, keyvals.shape[1]), lambda i: (at, 0))
    edges = [(EDGE, KV_COLS), (EDGE, (KEY_VALUE_HEADS - 1) * KV_COLS)]
    return pl.pallas_call(
        prepare_kernel,
        grid=(1,),
        in_specs=[smem] * 3 + [rows(1), rows(2)],
        out_specs=[smem] * 2 + [pl.BlockSpec(shape, lambda i: (0, 0)) for shape in edges],
        out_shape=[jax.ShapeDtypeStruct((1,), jnp.int32), jax.ShapeDtypeStruct((DOCS,), jnp.int32)]
        + [jax.ShapeDtypeStruct(shape, BF16) for shape in edges],
        compiler_params=pltpu.CompilerParams(vmem_limit_bytes=VMEM_BYTES),
        name="prepare",
    )(me, starts, partner, keyvals, keyvals)


def fill_bias(bias, info_ref):
    def doc(position):
        return sum((position >= info_ref[piece]).astype(jnp.int32) for piece in range(1, DOCS))

    key = lax.broadcasted_iota(jnp.int32, (EDGE, 1), 0) + HEAD_ROWS
    query = lax.broadcasted_iota(jnp.int32, (1, TOK_DEV), 1)
    bias[0:EDGE] = jnp.where((key >= info_ref[0]) & (query < info_ref[1]), 0.0, MASKED)
    key = lax.broadcasted_iota(jnp.int32, (TOK_DEV, 1), 0)
    bias[EDGE:ROWS] = jnp.where((doc(key) == doc(query)) & (key <= query), 0.0, MASKED)


def grads_of(keys, values, q, g, norm, delta, bias):
    s = mul_nt(keys, q)
    dp = mul_nt(values, g)
    p = jnp.exp2((s * (SCALE * LOG2E) - norm) + bias)
    return p.astype(BF16), (p * (dp - delta)).astype(BF16)


def twice(x):
    return jnp.concatenate([x, x], 1)


EARLY = slice(0, HEAD_ROWS)
LATE = slice(HEAD_ROWS, TOK_DEV)


def group_kernel(older, *refs):
    info_ref, q_ref, g_ref, l_ref, d_ref, edge_k_ref, edge_v_ref, k_ref, v_ref = refs[:9]
    out_ref, swap_ref, late_grad_ref, bias, keys_t, total, p_late, s_late, p_early, s_early = refs[-10:]
    step = pl.program_id(0)
    place = lax.rem(step, PAIRS)
    out_cols = [pl.ds(pl.multiple_of((2 * place + j) * HEAD_SIZE, HEAD_SIZE), HEAD_SIZE) for j in range(2)]

    @pl.when(step == 0)
    def _():
        fill_bias(bias, info_ref)
        if older:
            swap_ref[:, 0 : older * KV_COLS] = refs[9][...]

    @pl.when(place == 0)
    def _():
        keys_t[:, 0:EDGE] = edge_k_ref[...].T
        keys_t[:, EDGE:ROWS] = k_ref[...].T
        total[...] = jnp.zeros_like(total)

    keys = jnp.concatenate([edge_k_ref[...], k_ref[...]], 0)
    values = jnp.concatenate([edge_v_ref[...], v_ref[...]], 0)

    def pair(ref, span):
        return jnp.concatenate([ref[span, cols(0)], ref[span, cols(1)]], 0)

    def pair_row(rows, span):
        return jnp.concatenate([rows[0][:, span], rows[1][:, span]], 1)

    norms = [l_ref[pl.ds(2 * place + j, 1), :] * LOG2E for j in range(2)]
    deltas = [d_ref[pl.ds(2 * place + j, 1), :] for j in range(2)]
    for j in range(2):
        q = q_ref[LATE, cols(j)]
        g = g_ref[LATE, cols(j)]
        columns = slice(j * WIDE, (j + 1) * WIDE)
        for low in range(0, ROWS, 128):
            span = slice(low, low + 128)
            p_late[span, columns], s_late[span, columns] = grads_of(
                keys[span], values[span], q, g, norms[j][:, LATE], deltas[j][:, LATE], bias[span, LATE]
            )
    q = pair(q_ref, EARLY)
    g = pair(g_ref, EARLY)
    for low in range(0, ROWS_TOP, 128):
        span = slice(low, low + 128)
        p_early[span], s_early[span] = grads_of(
            keys[span], values[span], q, g, pair_row(norms, EARLY), pair_row(deltas, EARLY), twice(bias[span, EARLY])
        )
    for j in range(2):
        x = mul_nn(keys_t[...], s_late[:, j * WIDE : (j + 1) * WIDE])
        out_ref[LATE, out_cols[j]] = (x.T * SCALE).astype(BF16)
    x = (mul_nn(keys_t[:, :ROWS_TOP], s_early[...]).T * SCALE).astype(BF16)
    out_ref[EARLY, out_cols[0]] = x[:HEAD_ROWS]
    out_ref[EARLY, out_cols[1]] = x[HEAD_ROWS:]
    for j, (late, early, ref) in enumerate(((s_late, s_early, q_ref), (p_late, p_early, g_ref))):
        total[:, cols(j)] += mul_nn(late[...], pair(ref, LATE))
        total[0:ROWS_TOP, cols(j)] += mul_nn(early[...], pair(ref, EARLY))

    @pl.when(place == PAIRS - 1)
    def _():
        group = lax.div(step, PAIRS) + older
        for j, scale in enumerate((SCALE, 1.0)):
            to_swap = pl.ds(pl.multiple_of(group * KV_COLS + j * HEAD_SIZE, HEAD_SIZE), HEAD_SIZE)
            swap_ref[:, to_swap] = (total[0:EDGE, cols(j)] * scale).astype(BF16)
            early = (total[EDGE:ROWS_TOP, cols(j)] * scale).astype(BF16)
            for at in range(FOLDS):
                out_ref[TOK_DEV:CHUNK_ROWS, cols(j * FOLDS + at)] = early[at * FOLD_ROWS : (at + 1) * FOLD_ROWS]
            late_grad_ref[:, cols(j)] = total[ROWS_TOP:ROWS, cols(j)] * scale


def group_grads(first, count, edge_at, info, q, g, norms, deltas, keyvals, edge, *older):
    group_of = lambda i: first + i // PAIRS
    pair_cols = pl.BlockSpec((TOK_DEV, 2 * HEAD_SIZE), lambda i: (0, first * PAIRS + i))
    rows = pl.BlockSpec((GROUP_HEADS, TOK_DEV), lambda i: (group_of(i), 0))
    part = lambda height, at: pl.BlockSpec((height, HEAD_SIZE), lambda i: (0, at(group_of(i))))
    whole = lambda *shape: pl.BlockSpec(shape, lambda i: (0, 0))
    in_specs = [
        pl.BlockSpec(memory_space=pltpu.SMEM),
        pair_cols,
        pair_cols,
        rows,
        rows,
        part(EDGE, lambda group: 2 * (group - edge_at)),
        part(EDGE, lambda group: 2 * (group - edge_at) + 1),
        part(TOK_DEV, lambda group: group),
        part(TOK_DEV, lambda group: KEY_VALUE_HEADS + group),
    ]
    operands = [info, q, g, norms, deltas, edge, edge, keyvals, keyvals, *older]
    in_specs += [whole(*block.shape) for block in older]
    earlier = sum(block.shape[1] for block in older) // KV_COLS
    swap = (EDGE, (earlier + count) * KV_COLS)
    return pl.pallas_call(
        functools.partial(group_kernel, earlier),
        grid=(count * PAIRS,),
        in_specs=in_specs,
        out_specs=[
            pl.BlockSpec((CHUNK_ROWS, GROUP_COLS), lambda i: (i // PAIRS, 0)),
            whole(*swap),
            pl.BlockSpec((EDGE, KV_COLS), lambda i: (0, i // PAIRS)),
        ],
        scratch_shapes=[
            pltpu.VMEM((ROWS, TOK_DEV), F32),
            pltpu.VMEM((HEAD_SIZE, ROWS), BF16),
            pltpu.VMEM((ROWS, KV_COLS), F32),
            pltpu.VMEM((ROWS, 2 * WIDE), BF16),
            pltpu.VMEM((ROWS, 2 * WIDE), BF16),
            pltpu.VMEM((ROWS_TOP, WIDE), BF16),
            pltpu.VMEM((ROWS_TOP, WIDE), BF16),
        ],
        out_shape=[
            jax.ShapeDtypeStruct((count * CHUNK_ROWS, GROUP_COLS), BF16),
            jax.ShapeDtypeStruct(swap, BF16),
            jax.ShapeDtypeStruct((EDGE, count * KV_COLS), F32),
        ],
        cost_estimate=pl.CostEstimate(flops=1 << 20, bytes_accessed=1 << 16, transcendentals=0),
        compiler_params=pltpu.CompilerParams(vmem_limit_bytes=VMEM_BYTES),
        name="group_grads",
    )(*operands)


def join_kernel(*refs):
    *own_refs, back_ref, out_ref = refs
    at = 0
    for own_ref in own_refs:
        columns = slice(at, at + own_ref.shape[1])
        out_ref[:, columns] = (own_ref[...] + back_ref[:, columns].astype(F32)).astype(BF16)
        at += own_ref.shape[1]


def join_grads(owns, back):
    return pl.pallas_call(
        join_kernel,
        out_shape=jax.ShapeDtypeStruct(back.shape, BF16),
        compiler_params=pltpu.CompilerParams(vmem_limit_bytes=VMEM_BYTES),
        name="join_grads",
    )(*owns, back)


def place_kernel(pieces, *refs):
    chunk_ref, out_ref, done = refs[-3:]
    copies = [
        pltpu.make_async_copy(chunk_ref.at[source], out_ref.at[0, *target], done.at[at])
        for at, (source, target) in enumerate(pieces)
    ]
    for copy in copies:
        copy.start()
    for copy in copies:
        copy.wait()


def place(total, chunk, pieces):
    operands = [chunk] if total is None else [total, chunk]
    vmem = pl.BlockSpec(memory_space=pltpu.VMEM)
    width = QUERY_HEADS * HEAD_SIZE + KEY_VALUE_HEADS * KV_COLS
    return pl.pallas_call(
        functools.partial(place_kernel, pieces),
        in_specs=[vmem] if total is None else [ANY, vmem],
        out_specs=ANY,
        out_shape=jax.ShapeDtypeStruct((1, TOK_DEV, width), chunk.dtype),
        input_output_aliases={} if total is None else {0: 0},
        scratch_shapes=[pltpu.SemaphoreType.DMA((len(pieces),))],
        compiler_params=pltpu.CompilerParams(vmem_limit_bytes=4 << 20),
        name="place",
    )(*operands)


def keyval_cols(part, group):
    return cols(QUERY_HEADS + part * KEY_VALUE_HEADS + group)


def place_chunk(total, chunk, first):
    pieces = []
    for row in range(0, chunk.shape[0], CHUNK_ROWS):
        group = first + row // CHUNK_ROWS
        rows = slice(0, TOK_DEV)
        pieces.append(
            (
                (slice(row, row + TOK_DEV), slice(0, GROUP_COLS)),
                (rows, slice(group * GROUP_COLS, (group + 1) * GROUP_COLS)),
            )
        )
        for part in range(2):
            for at in range(FOLDS):
                source = (slice(row + TOK_DEV, row + CHUNK_ROWS), cols(part * FOLDS + at))
                pieces.append((source, (slice(at * FOLD_ROWS, (at + 1) * FOLD_ROWS), keyval_cols(part, group))))
    return place(total, chunk, pieces)


def place_late(total, chunk, groups):
    pieces = []
    for at, group in enumerate(groups):
        for part in range(2):
            pieces.append(((slice(0, EDGE), cols(2 * at + part)), (LATE, keyval_cols(part, group))))
    return place(total, chunk, pieces)


def local(q_heads, key_value_heads, grad_out, log_norm, row_delta, doc_starts, partner):
    queries, outgrads, keyvals = q_heads[0], grad_out[0], key_value_heads[0]
    norms, deltas = log_norm[0], row_delta[0]
    ctx = lax.axis_size("ctx")
    assert ctx == 1 << DIGITS
    pipe = lax.axis_size("pipe")
    me = lax.axis_index("ctx").astype(jnp.int32)[None]
    digit, info, first_rows, other_rows = prepare(me, doc_starts[0].T, partner, keyvals)

    def stage(rows, work=None, *operands):
        def branch(bit):
            def run(rows, *operands):
                arrived = lax.ppermute(rows, "ctx", [(low, low ^ 1 << bit) for low in range(ctx)])
                return arrived, group_grads(*work, *operands) if work else []

            return run

        return lax.switch(digit[0], [branch(bit) for bit in range(DIGITS)], rows, *operands)

    def to_previous(chunk):
        return lax.ppermute(chunk, "pipe", [(source, (source - 1) % pipe) for source in range(pipe)])

    common = (info, queries, outgrads, norms, deltas, keyvals)
    edge, _ = stage(first_rows)
    edges, (chunk, swap, own) = stage(other_rows, (0, 1, 0), *common, edge)
    sent, owns = [to_previous(chunk)], [own]
    for group in range(1, KEY_VALUE_HEADS):
        chunk, swap, own = group_grads(group, 1, 1, *common, edges, swap)
        sent.append(to_previous(chunk))
        owns.append(own)
    back, _ = stage(swap)
    late_grad = to_previous(join_grads(owns, back))
    total = None
    for group, chunk in enumerate(sent):
        total = place_chunk(total, chunk, group)
    return place_late(total, late_grad, range(KEY_VALUE_HEADS))


def solution(mesh):
    in_specs = (
        P("pipe", "ctx", None),
        P("pipe", "ctx", None),
        P("pipe", "ctx", None),
        P("pipe", None, "ctx"),
        P("pipe", None, "ctx"),
        P("pipe", None, None),
        P("pipe", None),
    )
    out_specs = P("pipe", "ctx", None)
    return jax.shard_map(local, mesh=mesh, in_specs=in_specs, out_specs=out_specs, check_vma=False)
```

```python
import functools
import math

import jax
import jax.numpy as jnp
from jax import lax
from jax.experimental import pallas as pl
from jax.experimental.pallas import tpu as pltpu
from jax.sharding import PartitionSpec as P

HEAD_SIZE = 128
QUERY_HEADS = 32
KEY_VALUE_HEADS = 4
TOK_DEV = 384
EDGE = 256
DOCS = 4

GROUP_HEADS = QUERY_HEADS // KEY_VALUE_HEADS
GROUP_COLS = GROUP_HEADS * HEAD_SIZE
KV_COLS = 2 * HEAD_SIZE
HEAD_ROWS = TOK_DEV - EDGE
WIDE = 256
ROWS = EDGE + TOK_DEV
ROWS_TOP = EDGE + HEAD_ROWS
PAIRS = GROUP_HEADS // 2
FOLDS = 4
FOLD_ROWS = HEAD_ROWS // FOLDS
CHUNK_ROWS = TOK_DEV + FOLD_ROWS
DIGITS = 6
SCALE = HEAD_SIZE**-0.5
LOG2E = math.log2(math.e)
MASKED = -1e30
VMEM_BYTES = 56 << 20
F32 = jnp.float32
BF16 = jnp.bfloat16
ANY = pl.BlockSpec(memory_space=pl.ANY)


def mul_nt(a, b):
    return lax.dot_general(a, b, (((1,), (1,)), ((), ())), preferred_element_type=F32)


def mul_nn(a, b):
    return lax.dot_general(a, b, (((1,), (0,)), ((), ())), preferred_element_type=F32)


def cols(head):
    return slice(head * HEAD_SIZE, (head + 1) * HEAD_SIZE)


def prepare_kernel(me_ref, starts_ref, partner_ref, top_ref, bottom_ref, digit_ref, info_ref, *edge_refs):
    me = me_ref[0]
    other = partner_ref[0, me]
    flipped = jnp.bitwise_xor(me, other)
    digit = jnp.int32(0)
    for bit in range(1, DIGITS):
        digit += jnp.where(flipped >= 1 << bit, 1, 0)
    digit_ref[0] = digit
    for piece in range(1, DOCS):
        info_ref[piece] = starts_ref[piece, me]
    info_ref[0] = starts_ref[DOCS - 1, other]
    for group in range(KEY_VALUE_HEADS):
        edge_ref = edge_refs[min(group, 1)]
        for part in range(2):
            source = cols(part * KEY_VALUE_HEADS + group)
            target = cols(2 * max(group - 1, 0) + part)
            edge_ref[0:HEAD_ROWS, target] = top_ref[:, source]
            edge_ref[HEAD_ROWS:EDGE, target] = bottom_ref[:, source]


def prepare(me, starts, partner, keyvals):
    smem = pl.BlockSpec(memory_space=pltpu.SMEM)
    rows = lambda at: pl.BlockSpec((HEAD_ROWS, keyvals.shape[1]), lambda i: (at, 0))
    edges = [(EDGE, KV_COLS), (EDGE, (KEY_VALUE_HEADS - 1) * KV_COLS)]
    return pl.pallas_call(
        prepare_kernel,
        grid=(1,),
        in_specs=[smem] * 3 + [rows(1), rows(2)],
        out_specs=[smem] * 2 + [pl.BlockSpec(shape, lambda i: (0, 0)) for shape in edges],
        out_shape=[jax.ShapeDtypeStruct((1,), jnp.int32), jax.ShapeDtypeStruct((DOCS,), jnp.int32)]
        + [jax.ShapeDtypeStruct(shape, BF16) for shape in edges],
        compiler_params=pltpu.CompilerParams(vmem_limit_bytes=VMEM_BYTES),
        name="prepare",
    )(me, starts, partner, keyvals, keyvals)


def fill_bias(bias, info_ref):
    def doc(position):
        return sum((position >= info_ref[piece]).astype(jnp.int32) for piece in range(1, DOCS))

    key = lax.broadcasted_iota(jnp.int32, (EDGE, 1), 0) + HEAD_ROWS
    query = lax.broadcasted_iota(jnp.int32, (1, TOK_DEV), 1)
    bias[0:EDGE] = jnp.where((key >= info_ref[0]) & (query < info_ref[1]), 0.0, MASKED)
    key = lax.broadcasted_iota(jnp.int32, (TOK_DEV, 1), 0)
    bias[EDGE:ROWS] = jnp.where((doc(key) == doc(query)) & (key <= query), 0.0, MASKED)


def grads_of(keys, values, q, g, norm, delta, bias):
    s = mul_nt(keys, q)
    dp = mul_nt(values, g)
    p = jnp.exp2((s * (SCALE * LOG2E) - norm) + bias)
    return p.astype(BF16), (p * (dp - delta)).astype(BF16)


def twice(x):
    return jnp.concatenate([x, x], 1)


EARLY = slice(0, HEAD_ROWS)
LATE = slice(HEAD_ROWS, TOK_DEV)


def group_kernel(group, *refs):
    info_ref, q_ref, g_ref, l_ref, d_ref, edge_k_ref, edge_v_ref, k_ref, v_ref = refs[:9]
    out_ref, early_ref, swap_ref, late_grad_ref, bias, keys_t, total, p_late, s_late, p_early, s_early = refs[-11:]
    step = pl.program_id(0)

    @pl.when(step == 0)
    def _():
        fill_bias(bias, info_ref)
        keys_t[:, 0:EDGE] = edge_k_ref[...].T
        keys_t[:, EDGE:ROWS] = k_ref[...].T
        total[...] = jnp.zeros_like(total)

    out_ref[TOK_DEV:CHUNK_ROWS] = refs[9][...] if group else jnp.zeros((FOLD_ROWS, 2 * HEAD_SIZE), BF16)

    keys = jnp.concatenate([edge_k_ref[...], k_ref[...]], 0)
    values = jnp.concatenate([edge_v_ref[...], v_ref[...]], 0)

    def pair(ref, span):
        return jnp.concatenate([ref[span, cols(0)], ref[span, cols(1)]], 0)

    def pair_row(rows, span):
        return jnp.concatenate([rows[0][:, span], rows[1][:, span]], 1)

    norms = [l_ref[pl.ds(2 * step + j, 1), :] * LOG2E for j in range(2)]
    deltas = [d_ref[pl.ds(2 * step + j, 1), :] for j in range(2)]
    for j in range(2):
        q = q_ref[LATE, cols(j)]
        g = g_ref[LATE, cols(j)]
        columns = slice(j * WIDE, (j + 1) * WIDE)
        for low in range(0, ROWS, 128):
            span = slice(low, low + 128)
            p_late[span, columns], s_late[span, columns] = grads_of(
                keys[span], values[span], q, g, norms[j][:, LATE], deltas[j][:, LATE], bias[span, LATE]
            )
    q = pair(q_ref, EARLY)
    g = pair(g_ref, EARLY)
    for low in range(0, ROWS_TOP, 128):
        span = slice(low, low + 128)
        p_early[span], s_early[span] = grads_of(
            keys[span], values[span], q, g, pair_row(norms, EARLY), pair_row(deltas, EARLY), twice(bias[span, EARLY])
        )
    for j in range(2):
        x = mul_nn(keys_t[...], s_late[:, j * WIDE : (j + 1) * WIDE])
        out_ref[LATE, cols(j)] = (x.T * SCALE).astype(BF16)
    x = (mul_nn(keys_t[:, :ROWS_TOP], s_early[...]).T * SCALE).astype(BF16)
    out_ref[EARLY, cols(0)] = x[:HEAD_ROWS]
    out_ref[EARLY, cols(1)] = x[HEAD_ROWS:]
    for j, (late, early, ref) in enumerate(((s_late, s_early, q_ref), (p_late, p_early, g_ref))):
        total[:, cols(j)] += mul_nn(late[...], pair(ref, LATE))
        total[0:ROWS_TOP, cols(j)] += mul_nn(early[...], pair(ref, EARLY))

    @pl.when(step == PAIRS - 1)
    def _():
        for j, scale in enumerate((SCALE, 1.0)):
            swap_ref[:, cols(j)] = (total[0:EDGE, cols(j)] * scale).astype(BF16)
            early = (total[EDGE:ROWS_TOP, cols(j)] * scale).astype(BF16)
            for at in range(FOLDS):
                early_ref[:, cols(j * FOLDS + at)] = early[at * FOLD_ROWS : (at + 1) * FOLD_ROWS]
            late_grad_ref[:, cols(j)] = total[ROWS_TOP:ROWS, cols(j)] * scale


def group_grads(group, edge_at, info, q, g, norms, deltas, keyvals, edge, *before):
    pair_cols = pl.BlockSpec((TOK_DEV, 2 * HEAD_SIZE), lambda i: (0, group * PAIRS + i))
    rows = pl.BlockSpec((GROUP_HEADS, TOK_DEV), lambda i: (group, 0))
    part = lambda height, at: pl.BlockSpec((height, HEAD_SIZE), lambda i: (0, at))
    whole = lambda *shape: pl.BlockSpec(shape, lambda i: (0, 0))
    in_specs = [
        pl.BlockSpec(memory_space=pltpu.SMEM),
        pair_cols,
        pair_cols,
        rows,
        rows,
        part(EDGE, 2 * (group - edge_at)),
        part(EDGE, 2 * (group - edge_at) + 1),
        part(TOK_DEV, group),
        part(TOK_DEV, KEY_VALUE_HEADS + group),
    ]
    operands = [info, q, g, norms, deltas, edge, edge, keyvals, keyvals, *before]
    if before:
        in_specs += [pl.BlockSpec((FOLD_ROWS, 2 * HEAD_SIZE), lambda i: (0, i)), ANY]
    return pl.pallas_call(
        functools.partial(group_kernel, group),
        grid=(PAIRS,),
        in_specs=in_specs,
        out_specs=[
            pl.BlockSpec((CHUNK_ROWS, 2 * HEAD_SIZE), lambda i: (0, i)),
            whole(FOLD_ROWS, GROUP_COLS),
            pl.BlockSpec((EDGE, KV_COLS), lambda i: (0, group)),
            whole(EDGE, KV_COLS),
        ],
        scratch_shapes=[
            pltpu.VMEM((ROWS, TOK_DEV), F32),
            pltpu.VMEM((HEAD_SIZE, ROWS), BF16),
            pltpu.VMEM((ROWS, KV_COLS), F32),
            pltpu.VMEM((ROWS, 2 * WIDE), BF16),
            pltpu.VMEM((ROWS, 2 * WIDE), BF16),
            pltpu.VMEM((ROWS_TOP, WIDE), BF16),
            pltpu.VMEM((ROWS_TOP, WIDE), BF16),
        ],
        out_shape=[
            jax.ShapeDtypeStruct((CHUNK_ROWS, GROUP_COLS), BF16),
            jax.ShapeDtypeStruct((FOLD_ROWS, GROUP_COLS), BF16),
            jax.ShapeDtypeStruct((EDGE, KEY_VALUE_HEADS * KV_COLS), BF16),
            jax.ShapeDtypeStruct((EDGE, KV_COLS), F32),
        ],
        input_output_aliases={len(operands) - 1: 2} if before else {},
        cost_estimate=pl.CostEstimate(flops=1 << 20, bytes_accessed=1 << 16, transcendentals=0),
        compiler_params=pltpu.CompilerParams(vmem_limit_bytes=VMEM_BYTES),
        name="group_grads",
    )(*operands)


def join_kernel(*refs):
    *own_refs, back_ref, early_ref, out_ref = refs
    for group, own_ref in enumerate(own_refs):
        columns = slice(group * KV_COLS, (group + 1) * KV_COLS)
        out_ref[0:EDGE, columns] = (own_ref[...] + back_ref[:, columns].astype(F32)).astype(BF16)
    out_ref[EDGE:] = early_ref[...]


def join_grads(owns, back, early):
    return pl.pallas_call(
        join_kernel,
        out_shape=jax.ShapeDtypeStruct((EDGE + FOLD_ROWS, GROUP_COLS), BF16),
        compiler_params=pltpu.CompilerParams(vmem_limit_bytes=VMEM_BYTES),
        name="join_grads",
    )(*owns, back, early)


def place_kernel(pieces, *refs):
    chunk_ref, out_ref, done = refs[-3:]
    copies = [
        pltpu.make_async_copy(chunk_ref.at[source], out_ref.at[0, *target], done.at[at])
        for at, (source, target) in enumerate(pieces)
    ]
    for copy in copies:
        copy.start()
    for copy in copies:
        copy.wait()


def place(total, chunk, pieces):
    operands = [chunk] if total is None else [total, chunk]
    vmem = pl.BlockSpec(memory_space=pltpu.VMEM)
    width = QUERY_HEADS * HEAD_SIZE + KEY_VALUE_HEADS * KV_COLS
    return pl.pallas_call(
        functools.partial(place_kernel, pieces),
        in_specs=[vmem] if total is None else [ANY, vmem],
        out_specs=ANY,
        out_shape=jax.ShapeDtypeStruct((1, TOK_DEV, width), chunk.dtype),
        input_output_aliases={} if total is None else {0: 0},
        scratch_shapes=[pltpu.SemaphoreType.DMA((len(pieces),))],
        compiler_params=pltpu.CompilerParams(vmem_limit_bytes=4 << 20),
        name="place",
    )(*operands)


def keyval_cols(part, group):
    return cols(QUERY_HEADS + part * KEY_VALUE_HEADS + group)


def folded_pieces(row, group):
    pieces = []
    for part in range(2):
        for at in range(FOLDS):
            source = (slice(row, row + FOLD_ROWS), cols(part * FOLDS + at))
            pieces.append((source, (slice(at * FOLD_ROWS, (at + 1) * FOLD_ROWS), keyval_cols(part, group))))
    return pieces


def place_chunk(total, chunk, group):
    rows = slice(0, TOK_DEV)
    pieces = [((rows, slice(0, GROUP_COLS)), (rows, slice(group * GROUP_COLS, (group + 1) * GROUP_COLS)))]
    if group:
        pieces += folded_pieces(TOK_DEV, group - 1)
    return place(total, chunk, pieces)


def place_late(total, chunk):
    pieces = folded_pieces(EDGE, KEY_VALUE_HEADS - 1)
    for group in range(KEY_VALUE_HEADS):
        for part in range(2):
            pieces.append(((slice(0, EDGE), cols(2 * group + part)), (LATE, keyval_cols(part, group))))
    return place(total, chunk, pieces)


def local(q_heads, key_value_heads, grad_out, log_norm, row_delta, doc_starts, partner):
    queries, outgrads, keyvals = q_heads[0], grad_out[0], key_value_heads[0]
    norms, deltas = log_norm[0], row_delta[0]
    ctx = lax.axis_size("ctx")
    assert ctx == 1 << DIGITS
    pipe = lax.axis_size("pipe")
    me = lax.axis_index("ctx").astype(jnp.int32)[None]
    digit, info, first_rows, other_rows = prepare(me, doc_starts[0].T, partner, keyvals)

    def stage(rows, work=None, *operands):
        def branch(bit):
            def run(rows, *operands):
                arrived = lax.ppermute(rows, "ctx", [(low, low ^ 1 << bit) for low in range(ctx)])
                return arrived, group_grads(*work, *operands) if work else []

            return run

        return lax.switch(digit[0], [branch(bit) for bit in range(DIGITS)], rows, *operands)

    def to_previous(chunk):
        return lax.ppermute(chunk, "pipe", [(source, (source - 1) % pipe) for source in range(pipe)])

    common = (info, queries, outgrads, norms, deltas, keyvals)
    edge, _ = stage(first_rows)
    edges, (chunk, early, swap, own) = stage(other_rows, (0, 0), *common, edge)
    sent, owns = [to_previous(chunk)], [own]
    for group in range(1, KEY_VALUE_HEADS):
        chunk, early, swap, own = group_grads(group, 1, *common, edges, early, swap)
        sent.append(to_previous(chunk))
        owns.append(own)
    back, _ = stage(swap)
    late_grad = to_previous(join_grads(owns, back, early))
    total = None
    for group, chunk in enumerate(sent):
        total = place_chunk(total, chunk, group)
    return place_late(total, late_grad)


def solution(mesh):
    in_specs = (
        P("pipe", "ctx", None),
        P("pipe", "ctx", None),
        P("pipe", "ctx", None),
        P("pipe", None, "ctx"),
        P("pipe", None, "ctx"),
        P("pipe", None, None),
        P("pipe", None),
    )
    out_specs = P("pipe", "ctx", None)
    return jax.shard_map(local, mesh=mesh, in_specs=in_specs, out_specs=out_specs, check_vma=False)
```

```python
import functools
import math

import jax
import jax.numpy as jnp
from jax import lax
from jax.experimental import pallas as pl
from jax.experimental.pallas import tpu as pltpu
from jax.sharding import PartitionSpec as P

HEAD_SIZE = 128
QUERY_HEADS = 32
KEY_VALUE_HEADS = 4
TOK_DEV = 384
EDGE = 256
DOCS = 4

GROUP_HEADS = QUERY_HEADS // KEY_VALUE_HEADS
GROUP_COLS = GROUP_HEADS * HEAD_SIZE
KV_COLS = 2 * HEAD_SIZE
HEAD_ROWS = TOK_DEV - EDGE
WIDE = 256
ROWS = EDGE + TOK_DEV
ROWS_TOP = EDGE + HEAD_ROWS
PAIRS = GROUP_HEADS // 2
FOLDS = 4
FOLD_ROWS = HEAD_ROWS // FOLDS
CHUNK_ROWS = TOK_DEV + FOLD_ROWS
DIGITS = 6
SIZES = (176, EDGE)
SCALE = HEAD_SIZE**-0.5
LOG2E = math.log2(math.e)
MASKED = -1e30
VMEM_BYTES = 56 << 20
F32 = jnp.float32
BF16 = jnp.bfloat16
ANY = pl.BlockSpec(memory_space=pl.ANY)


def mul_nt(a, b):
    return lax.dot_general(a, b, (((1,), (1,)), ((), ())), preferred_element_type=F32)


def mul_nn(a, b):
    return lax.dot_general(a, b, (((1,), (0,)), ((), ())), preferred_element_type=F32)


def cols(head):
    return slice(head * HEAD_SIZE, (head + 1) * HEAD_SIZE)


def prepare_kernel(me_ref, starts_ref, partner_ref, top_ref, bottom_ref, digit_ref, back_ref, info_ref, *edge_refs):
    me = me_ref[0]
    other = partner_ref[0, me]
    flipped = jnp.bitwise_xor(me, other)
    digit = jnp.int32(0)
    for bit in range(1, DIGITS):
        digit += jnp.where(flipped >= 1 << bit, 1, 0)
    digit_ref[0] = digit
    tail = TOK_DEV - jnp.minimum(starts_ref[DOCS - 1, me], starts_ref[DOCS - 1, other])
    back_ref[0] = digit * len(SIZES) + jnp.where(tail > SIZES[0], 1, 0)
    for piece in range(1, DOCS):
        info_ref[piece] = starts_ref[piece, me]
    info_ref[0] = starts_ref[DOCS - 1, other]
    for group in range(KEY_VALUE_HEADS):
        edge_ref = edge_refs[min(group, 1)]
        for part in range(2):
            source = cols(part * KEY_VALUE_HEADS + group)
            target = cols(2 * max(group - 1, 0) + part)
            edge_ref[0:HEAD_ROWS, target] = top_ref[:, source]
            edge_ref[HEAD_ROWS:EDGE, target] = bottom_ref[:, source]


def prepare(me, starts, partner, keyvals):
    smem = pl.BlockSpec(memory_space=pltpu.SMEM)
    rows = lambda at: pl.BlockSpec((HEAD_ROWS, keyvals.shape[1]), lambda i: (at, 0))
    edges = [(EDGE, KV_COLS), (EDGE, (KEY_VALUE_HEADS - 1) * KV_COLS)]
    return pl.pallas_call(
        prepare_kernel,
        grid=(1,),
        in_specs=[smem] * 3 + [rows(1), rows(2)],
        out_specs=[smem] * 3 + [pl.BlockSpec(shape, lambda i: (0, 0)) for shape in edges],
        out_shape=[jax.ShapeDtypeStruct((size,), jnp.int32) for size in (1, 1, DOCS)]
        + [jax.ShapeDtypeStruct(shape, BF16) for shape in edges],
        compiler_params=pltpu.CompilerParams(vmem_limit_bytes=VMEM_BYTES),
        name="prepare",
    )(me, starts, partner, keyvals, keyvals)


def fill_bias(bias, info_ref):
    def doc(position):
        return sum((position >= info_ref[piece]).astype(jnp.int32) for piece in range(1, DOCS))

    key = lax.broadcasted_iota(jnp.int32, (EDGE, 1), 0) + HEAD_ROWS
    query = lax.broadcasted_iota(jnp.int32, (1, TOK_DEV), 1)
    bias[0:EDGE] = jnp.where((key >= info_ref[0]) & (query < info_ref[1]), 0.0, MASKED)
    key = lax.broadcasted_iota(jnp.int32, (TOK_DEV, 1), 0)
    bias[EDGE:ROWS] = jnp.where((doc(key) == doc(query)) & (key <= query), 0.0, MASKED)


def grads_of(keys, values, q, g, norm, delta, bias):
    s = mul_nt(keys, q)
    dp = mul_nt(values, g)
    p = jnp.exp2((s * (SCALE * LOG2E) - norm) + bias)
    return p.astype(BF16), (p * (dp - delta)).astype(BF16)


def twice(x):
    return jnp.concatenate([x, x], 1)


EARLY = slice(0, HEAD_ROWS)
LATE = slice(HEAD_ROWS, TOK_DEV)


def group_kernel(older, *refs):
    info_ref, q_ref, g_ref, l_ref, d_ref, edge_k_ref, edge_v_ref, k_ref, v_ref = refs[:9]
    out_ref, swap_ref, late_grad_ref, bias, keys_t, total, p_late, s_late, p_early, s_early = refs[-10:]
    step = pl.program_id(0)
    place = lax.rem(step, PAIRS)
    out_cols = [pl.ds(pl.multiple_of((2 * place + j) * HEAD_SIZE, HEAD_SIZE), HEAD_SIZE) for j in range(2)]

    @pl.when(step == 0)
    def _():
        fill_bias(bias, info_ref)
        if older:
            swap_ref[:, 0 : older * KV_COLS] = refs[9][...]

    @pl.when(place == 0)
    def _():
        keys_t[:, 0:EDGE] = edge_k_ref[...].T
        keys_t[:, EDGE:ROWS] = k_ref[...].T
        total[...] = jnp.zeros_like(total)

    keys = jnp.concatenate([edge_k_ref[...], k_ref[...]], 0)
    values = jnp.concatenate([edge_v_ref[...], v_ref[...]], 0)

    def pair(ref, span):
        return jnp.concatenate([ref[span, cols(0)], ref[span, cols(1)]], 0)

    def pair_row(rows, span):
        return jnp.concatenate([rows[0][:, span], rows[1][:, span]], 1)

    norms = [l_ref[pl.ds(2 * place + j, 1), :] * LOG2E for j in range(2)]
    deltas = [d_ref[pl.ds(2 * place + j, 1), :] for j in range(2)]
    for j in range(2):
        q = q_ref[LATE, cols(j)]
        g = g_ref[LATE, cols(j)]
        columns = slice(j * WIDE, (j + 1) * WIDE)
        for low in range(0, ROWS, 128):
            span = slice(low, low + 128)
            p_late[span, columns], s_late[span, columns] = grads_of(
                keys[span], values[span], q, g, norms[j][:, LATE], deltas[j][:, LATE], bias[span, LATE]
            )
    q = pair(q_ref, EARLY)
    g = pair(g_ref, EARLY)
    for low in range(0, ROWS_TOP, 128):
        span = slice(low, low + 128)
        p_early[span], s_early[span] = grads_of(
            keys[span], values[span], q, g, pair_row(norms, EARLY), pair_row(deltas, EARLY), twice(bias[span, EARLY])
        )
    for j in range(2):
        x = mul_nn(keys_t[...], s_late[:, j * WIDE : (j + 1) * WIDE])
        out_ref[LATE, out_cols[j]] = (x.T * SCALE).astype(BF16)
    x = (mul_nn(keys_t[:, :ROWS_TOP], s_early[...]).T * SCALE).astype(BF16)
    out_ref[EARLY, out_cols[0]] = x[:HEAD_ROWS]
    out_ref[EARLY, out_cols[1]] = x[HEAD_ROWS:]
    for j, (late, early, ref) in enumerate(((s_late, s_early, q_ref), (p_late, p_early, g_ref))):
        total[:, cols(j)] += mul_nn(late[...], pair(ref, LATE))
        total[0:ROWS_TOP, cols(j)] += mul_nn(early[...], pair(ref, EARLY))

    @pl.when(place == PAIRS - 1)
    def _():
        group = lax.div(step, PAIRS) + older
        for j, scale in enumerate((SCALE, 1.0)):
            to_swap = pl.ds(pl.multiple_of(group * KV_COLS + j * HEAD_SIZE, HEAD_SIZE), HEAD_SIZE)
            swap_ref[:, to_swap] = (total[0:EDGE, cols(j)] * scale).astype(BF16)
            early = (total[EDGE:ROWS_TOP, cols(j)] * scale).astype(BF16)
            for at in range(FOLDS):
                out_ref[TOK_DEV:CHUNK_ROWS, cols(j * FOLDS + at)] = early[at * FOLD_ROWS : (at + 1) * FOLD_ROWS]
            late_grad_ref[:, cols(j)] = total[ROWS_TOP:ROWS, cols(j)] * scale


def group_grads(first, count, edge_at, info, q, g, norms, deltas, keyvals, edge, *older):
    group_of = lambda i: first + i // PAIRS
    pair_cols = pl.BlockSpec((TOK_DEV, 2 * HEAD_SIZE), lambda i: (0, first * PAIRS + i))
    rows = pl.BlockSpec((GROUP_HEADS, TOK_DEV), lambda i: (group_of(i), 0))
    part = lambda height, at: pl.BlockSpec((height, HEAD_SIZE), lambda i: (0, at(group_of(i))))
    whole = lambda *shape: pl.BlockSpec(shape, lambda i: (0, 0))
    in_specs = [
        pl.BlockSpec(memory_space=pltpu.SMEM),
        pair_cols,
        pair_cols,
        rows,
        rows,
        part(EDGE, lambda group: 2 * (group - edge_at)),
        part(EDGE, lambda group: 2 * (group - edge_at) + 1),
        part(TOK_DEV, lambda group: group),
        part(TOK_DEV, lambda group: KEY_VALUE_HEADS + group),
    ]
    operands = [info, q, g, norms, deltas, edge, edge, keyvals, keyvals, *older]
    in_specs += [whole(*block.shape) for block in older]
    earlier = sum(block.shape[1] for block in older) // KV_COLS
    swap = (EDGE, (earlier + count) * KV_COLS)
    return pl.pallas_call(
        functools.partial(group_kernel, earlier),
        grid=(count * PAIRS,),
        in_specs=in_specs,
        out_specs=[
            pl.BlockSpec((CHUNK_ROWS, GROUP_COLS), lambda i: (i // PAIRS, 0)),
            whole(*swap),
            pl.BlockSpec((EDGE, KV_COLS), lambda i: (0, i // PAIRS)),
        ],
        scratch_shapes=[
            pltpu.VMEM((ROWS, TOK_DEV), F32),
            pltpu.VMEM((HEAD_SIZE, ROWS), BF16),
            pltpu.VMEM((ROWS, KV_COLS), F32),
            pltpu.VMEM((ROWS, 2 * WIDE), BF16),
            pltpu.VMEM((ROWS, 2 * WIDE), BF16),
            pltpu.VMEM((ROWS_TOP, WIDE), BF16),
            pltpu.VMEM((ROWS_TOP, WIDE), BF16),
        ],
        out_shape=[
            jax.ShapeDtypeStruct((count * CHUNK_ROWS, GROUP_COLS), BF16),
            jax.ShapeDtypeStruct(swap, BF16),
            jax.ShapeDtypeStruct((EDGE, count * KV_COLS), F32),
        ],
        cost_estimate=pl.CostEstimate(flops=1 << 20, bytes_accessed=1 << 16, transcendentals=0),
        compiler_params=pltpu.CompilerParams(vmem_limit_bytes=VMEM_BYTES),
        name="group_grads",
    )(*operands)


def join_kernel(*refs):
    *own_refs, back_ref, out_ref = refs
    at = 0
    for own_ref in own_refs:
        columns = slice(at, at + own_ref.shape[1])
        out_ref[:, columns] = (own_ref[...] + back_ref[:, columns].astype(F32)).astype(BF16)
        at += own_ref.shape[1]


def join_grads(owns, back):
    return pl.pallas_call(
        join_kernel,
        out_shape=jax.ShapeDtypeStruct(back.shape, BF16),
        compiler_params=pltpu.CompilerParams(vmem_limit_bytes=VMEM_BYTES),
        name="join_grads",
    )(*owns, back)


def place_kernel(pieces, *refs):
    chunk_ref, out_ref, done = refs[-3:]
    copies = [
        pltpu.make_async_copy(chunk_ref.at[source], out_ref.at[0, *target], done.at[at])
        for at, (source, target) in enumerate(pieces)
    ]
    for copy in copies:
        copy.start()
    for copy in copies:
        copy.wait()


def place(total, chunk, pieces):
    operands = [chunk] if total is None else [total, chunk]
    vmem = pl.BlockSpec(memory_space=pltpu.VMEM)
    width = QUERY_HEADS * HEAD_SIZE + KEY_VALUE_HEADS * KV_COLS
    return pl.pallas_call(
        functools.partial(place_kernel, pieces),
        in_specs=[vmem] if total is None else [ANY, vmem],
        out_specs=ANY,
        out_shape=jax.ShapeDtypeStruct((1, TOK_DEV, width), chunk.dtype),
        input_output_aliases={} if total is None else {0: 0},
        scratch_shapes=[pltpu.SemaphoreType.DMA((len(pieces),))],
        compiler_params=pltpu.CompilerParams(vmem_limit_bytes=4 << 20),
        name="place",
    )(*operands)


def keyval_cols(part, group):
    return cols(QUERY_HEADS + part * KEY_VALUE_HEADS + group)


def place_chunk(total, chunk, first):
    pieces = []
    for row in range(0, chunk.shape[0], CHUNK_ROWS):
        group = first + row // CHUNK_ROWS
        rows = slice(0, TOK_DEV)
        pieces.append(
            (
                (slice(row, row + TOK_DEV), slice(0, GROUP_COLS)),
                (rows, slice(group * GROUP_COLS, (group + 1) * GROUP_COLS)),
            )
        )
        for part in range(2):
            for at in range(FOLDS):
                source = (slice(row + TOK_DEV, row + CHUNK_ROWS), cols(part * FOLDS + at))
                pieces.append((source, (slice(at * FOLD_ROWS, (at + 1) * FOLD_ROWS), keyval_cols(part, group))))
    return place(total, chunk, pieces)


def place_late(total, chunk, groups):
    pieces = []
    for at, group in enumerate(groups):
        for part in range(2):
            pieces.append(((slice(0, EDGE), cols(2 * at + part)), (LATE, keyval_cols(part, group))))
    return place(total, chunk, pieces)


def local(q_heads, key_value_heads, grad_out, log_norm, row_delta, doc_starts, partner):
    queries, outgrads, keyvals = q_heads[0], grad_out[0], key_value_heads[0]
    norms, deltas = log_norm[0], row_delta[0]
    ctx = lax.axis_size("ctx")
    assert ctx == 1 << DIGITS
    pipe = lax.axis_size("pipe")
    me = lax.axis_index("ctx").astype(jnp.int32)[None]
    digit, back_at, info, first_rows, other_rows = prepare(me, doc_starts[0].T, partner, keyvals)

    def stage(rows, work=None, *operands):
        def branch(bit):
            def run(rows, *operands):
                arrived = lax.ppermute(rows, "ctx", [(low, low ^ 1 << bit) for low in range(ctx)])
                return arrived, group_grads(*work, *operands) if work else []

            return run

        return lax.switch(digit[0], [branch(bit) for bit in range(DIGITS)], rows, *operands)

    def give_back(rows):
        def branch(bit, size):
            def run(rows):
                arrived = lax.ppermute(rows[EDGE - size :], "ctx", [(low, low ^ 1 << bit) for low in range(ctx)])
                return jnp.pad(arrived, ((EDGE - size, 0), (0, 0)))

            return run

        return lax.switch(back_at[0], [branch(bit, size) for bit in range(DIGITS) for size in SIZES], rows)

    def to_previous(chunk):
        return lax.ppermute(chunk, "pipe", [(source, (source - 1) % pipe) for source in range(pipe)])

    common = (info, queries, outgrads, norms, deltas, keyvals)
    edge, _ = stage(first_rows)
    edges, (chunk, swap, own) = stage(other_rows, (0, 1, 0), *common, edge)
    sent, owns = [to_previous(chunk)], [own]
    for group in range(1, KEY_VALUE_HEADS):
        chunk, swap, own = group_grads(group, 1, 1, *common, edges, swap)
        sent.append(to_previous(chunk))
        owns.append(own)
    back = give_back(swap)
    late_grad = to_previous(join_grads(owns, back))
    total = None
    for group, chunk in enumerate(sent):
        total = place_chunk(total, chunk, group)
    return place_late(total, late_grad, range(KEY_VALUE_HEADS))


def solution(mesh):
    in_specs = (
        P("pipe", "ctx", None),
        P("pipe", "ctx", None),
        P("pipe", "ctx", None),
        P("pipe", None, "ctx"),
        P("pipe", None, "ctx"),
        P("pipe", None, None),
        P("pipe", None),
    )
    out_specs = P("pipe", "ctx", None)
    return jax.shard_map(local, mesh=mesh, in_specs=in_specs, out_specs=out_specs, check_vma=False)
```
